128 devices in a mesh: col: 16 (over y, z_lo, core), row: 8 (over x, z_hi).
Axes of the slice: x: 4, y: 4, z: 4 (z_hi: 2, z_lo: 2; z = z_hi * 2 + z_lo), core: 2. Of those that a mesh axis runs over, the one named last changes fastest.
Arguments:
- pressure: float32 [256, 128, 128], P('col', 'row'), may hold values from -1 to 1
- water_sat: float32 [256, 128, 128], P('col', 'row'), may hold values from 0.1 to 0.35
- gas_sat: float32 [256, 128, 128], P('col', 'row'), may hold values from 0.05 to 0.3
- depth: float32 [256, 128, 128], P('col', 'row'), may hold values from 0 to 4
- pore_volume: float32 [256, 128, 128], P('col', 'row'), may hold values from 0.5 to 5
- old_mass: float32 [3, 256, 128, 128], P(None, 'col', 'row'), may hold values from 0.2 to 4
- transmissibility: float32 [3, 256, 128, 128], P(None, 'col', 'row'), may hold values from 0.5 to 5
- fault_column: int32 [128, 3, 3, 1024], P(('col', 'row')), may hold values from 0 to 255
- fault_layer: int32 [128, 3, 3, 1024], P(('col', 'row')), may hold values from 0 to 127
- fault_transmissibility: float32 [128, 3, 3, 1024], P(('col', 'row')), may hold values from 0 to 5, as said below
- perforation_cell: int32 [128, 128], P(('col', 'row')), may hold values from 0 to 32767
- well_index: float32 [128, 128], P(('col', 'row')), may hold values from 0.5 to 5
- well_pressure: float32 [128, 128], P(('col', 'row')), may hold values from -2 to 2
Outputs:
- residual: float32 [3, 256, 128, 128], P(None, 'col', 'row')
- diagonal_block: bfloat16 [9, 256, 128, 128], P(None, 'col', 'row')
- face_blocks: bfloat16 [3, 2, 9, 256, 128, 128], P(None, None, None, 'col', 'row')
- fault_blocks: bfloat16 [9, 128, 3, 3, 1024], P(None, ('col', 'row'))
- pressure_update: float32 [256, 128, 128], P('col', 'row')
The draws below stay inside these ranges and needn't reach their ends.
Inputs may be any that keep to these rules, and one draw needn't show every extreme that they name: fault_transmissibility[d, di + 1, dj + 1, k] equals fault_transmissibility[s, 1 - di, 1 - dj, k] for s the block at offset (di, dj); in each pair's slots the used ones come first and the rest are zero; only blocks beside each other (offsets of at most one along each areal dimension) share connections; every pair of such blocks uses 1024 // 2 or more slots, and some block uses all 1024 slots with every block beside it.
All inputs are finite; a program needn't handle non-finite values.
Results may differ from the reference program's by a relative error of at most 0.001.
Values sent between devices are 32-bit elements; how exact they have to be, the bound alone decides.
A program may use at most 192 MiB of HBM per device.

```python
import math
import jax
import jax.numpy as jnp
from jax import lax

CI = 16
CJ = 16
NZ = 128
SLOTS = 1024
PERF = 128
GI = 16
GJ = 8
OWNERS = 128
NI = 256
NJ = 128
CELLS = 32768


def partner_view_drawn(values):
    padded = jnp.pad(values, ((1, 1), (1, 1), (0, 0), (0, 0), (0, 0)))
    lines = []
    for first_offset in range(3):
        entries = []
        for second_offset in range(3):
            entries.append(padded[first_offset:first_offset + GI, second_offset:second_offset + GJ, 2 - first_offset, 2 - second_offset])
        lines.append(jnp.stack(entries, axis=2))
    return jnp.stack(lines, axis=2)


def draw_fault_transmissibility(key, part):
    key = jax.random.fold_in(key, 7)
    count_key = jax.random.fold_in(key, 1)
    heavy_key = jax.random.fold_in(key, 2)
    value_key = jax.random.fold_in(key, 3)
    block_i = lax.broadcasted_iota(jnp.int32, (GI, GJ, 3, 3, 1), 0)
    block_j = lax.broadcasted_iota(jnp.int32, (GI, GJ, 3, 3, 1), 1)
    offset_i = lax.broadcasted_iota(jnp.int32, (GI, GJ, 3, 3, 1), 2) - 1
    offset_j = lax.broadcasted_iota(jnp.int32, (GI, GJ, 3, 3, 1), 3) - 1
    partner_i = block_i + offset_i
    partner_j = block_j + offset_j
    inside = (partner_i >= 0) & (partner_i < GI) & (partner_j >= 0) & (partner_j < GJ)
    inside = inside & ((offset_i != 0) | (offset_j != 0))
    owner = block_i * GJ + block_j
    partner = partner_i * GJ + partner_j
    raw = jax.random.randint(count_key, (GI, GJ, 3, 3, 1), SLOTS // 2, SLOTS + 1)
    counts = jnp.where(owner < partner, raw, partner_view_drawn(raw))
    heavy = jax.random.randint(heavy_key, (), 0, OWNERS)
    counts = jnp.where((owner == heavy) | (partner == heavy), SLOTS, counts)
    counts = jnp.where(inside, counts, 0)
    slot = lax.broadcasted_iota(jnp.int32, (GI, GJ, 3, 3, SLOTS), 4)
    live = slot < counts
    values = jnp.exp(jax.random.uniform(value_key, (GI, GJ, 3, 3, SLOTS), jnp.float32, math.log(0.5), math.log(5.0)))
    mirrored = jnp.where(owner < partner, values, partner_view_drawn(values))
    return jnp.where(live, mirrored, 0.0).astype(jnp.float32).reshape(OWNERS, 3, 3, SLOTS)


def touch_ends(array, key, least, largest):
    spot = [jax.random.randint(jax.random.fold_in(key, axis), (), 0, length) for axis, length in enumerate(array.shape)]
    main_axis = array.shape.index(max(array.shape))
    beside = spot[:main_axis] + [(spot[main_axis] + 1) % array.shape[main_axis]] + spot[main_axis + 1:]
    return array.at[tuple(spot)].set(least).at[tuple(beside)].set(largest)


def block_levels(stream_key, shape, cuts, least, top_value):
    factor_of = 1.0
    for dim, shards_of in cuts:
        draws = jax.random.uniform(jax.random.fold_in(jax.random.fold_in(stream_key, 6), dim), (shards_of,), jnp.float32, least / len(cuts), top_value / len(cuts))
        factor_of = factor_of * jnp.repeat(jnp.exp(draws), shape[dim] // shards_of).reshape((-1,) + (1,) * (len(shape) - 1 - dim))
    return factor_of


def setup_inputs(seed: int = 0) -> dict:
    streams_of = jax.random.split(jax.random.key(seed), 14)
    pressure = jnp.clip(jax.random.uniform(streams_of[0], (NI, NJ, NZ), jnp.float32, -1.0, 1.0) * block_levels(streams_of[0], (NI, NJ, NZ), ((0, 16), (1, 8)), -0.4, 0.0), -1.0, 1.0)
    water_sat = jnp.clip(0.1 + 0.25 * jax.random.uniform(streams_of[1], (NI, NJ, NZ), jnp.float32) ** block_levels(streams_of[1], (NI, NJ, NZ), ((0, 16), (1, 8)), -0.2, 0.2), 0.1, 0.35)
    gas_sat = jnp.clip(0.05 + 0.25 * jax.random.uniform(streams_of[2], (NI, NJ, NZ), jnp.float32) ** block_levels(streams_of[2], (NI, NJ, NZ), ((0, 16), (1, 8)), -0.2, 0.2), 0.05, 0.3)
    depth = jnp.clip(4.0 * jax.random.uniform(streams_of[3], (NI, NJ, NZ), jnp.float32) ** block_levels(streams_of[3], (NI, NJ, NZ), ((0, 16), (1, 8)), -0.2, 0.2), 0.0, 4.0)
    pore_volume = jnp.clip(jnp.exp(math.log(5.0) - 2.3025851 * jax.random.uniform(streams_of[4], (NI, NJ, NZ), jnp.float32) ** block_levels(streams_of[4], (NI, NJ, NZ), ((0, 16), (1, 8)), -0.2, 0.2)), 0.5, 5.0)
    old_mass = jnp.clip(jnp.exp(math.log(4.0) - 2.9957323 * jax.random.uniform(streams_of[5], (3, NI, NJ, NZ), jnp.float32) ** block_levels(streams_of[5], (3, NI, NJ, NZ), ((1, 16), (2, 8)), -0.2, 0.2)), 0.2, 4.0)
    transmissibility = jnp.clip(jnp.exp(math.log(5.0) - 2.3025851 * jax.random.uniform(streams_of[6], (3, NI, NJ, NZ), jnp.float32) ** block_levels(streams_of[6], (3, NI, NJ, NZ), ((1, 16), (2, 8)), -0.2, 0.2)), 0.5, 5.0)
    fault_column = touch_ends(jax.random.randint(streams_of[7], (OWNERS, 3, 3, SLOTS), 0, CI * CJ), jax.random.fold_in(streams_of[7], 1), 0, (CI * CJ) - 1).astype(jnp.int32)
    fault_layer = touch_ends(jax.random.randint(streams_of[8], (OWNERS, 3, 3, SLOTS), 0, NZ), jax.random.fold_in(streams_of[8], 1), 0, NZ - 1).astype(jnp.int32)
    fault_transmissibility = draw_fault_transmissibility(jax.random.fold_in(streams_of[13], 71), 0)
    perforation_cell = touch_ends(jax.random.randint(streams_of[10], (OWNERS, PERF), 0, CI * CJ * NZ), jax.random.fold_in(streams_of[10], 1), 0, (CI * CJ * NZ) - 1).astype(jnp.int32)
    well_index = jnp.clip(jnp.exp(math.log(5.0) - 2.3025851 * jax.random.uniform(streams_of[11], (OWNERS, PERF), jnp.float32) ** block_levels(streams_of[11], (OWNERS, PERF), ((0, 128),), -0.2, 0.2)), 0.5, 5.0)
    well_pressure = jnp.clip(jax.random.uniform(streams_of[12], (OWNERS, PERF), jnp.float32, -2.0, 2.0) * block_levels(streams_of[12], (OWNERS, PERF), ((0, 128),), -0.4, 0.0), -2.0, 2.0)
    return {"pressure": pressure, "water_sat": water_sat, "gas_sat": gas_sat, "depth": depth, "pore_volume": pore_volume, "old_mass": old_mass, "transmissibility": transmissibility, "fault_column": fault_column, "fault_layer": fault_layer, "fault_transmissibility": fault_transmissibility, "perforation_cell": perforation_cell, "well_index": well_index, "well_pressure": well_pressure}


compress_water = 0.05
compress_oil = 0.1
compress_gas = 0.4
compress_rock = 0.02
solution_base = 0.5
solution_slope = 0.2
viscous_water = 0.3
viscous_oil = 0.8
viscous_gas = 0.05
gravity_water = 0.1
gravity_oil = 0.08
gravity_gas = 0.02
time_step = 0.5

def mobilities(press, water, gas):
    oil = 1.0 - water - gas
    mover_water = (1.0 + compress_water * press) * water * water / viscous_water
    mover_oil = (1.0 + compress_oil * press) * oil * oil / viscous_oil
    mover_gas = (1.0 + compress_gas * press) * gas * gas / viscous_gas
    mover_solved = (solution_base + solution_slope * press) * mover_oil
    return (mover_water, mover_oil, mover_gas, mover_solved, mover_water + mover_oil + mover_gas + mover_solved)

def unit_rows(values, pullback):
    zeros = jnp.zeros_like(values[0])
    ones = jnp.ones_like(values[0])
    rows = []
    for target in range(3):
        rows.append(pullback(tuple((ones if other == target else zeros for other in range(3)))))
    return rows

def pick_block(rows, offset):
    return jnp.stack([rows[equation][offset + unknown] for equation in range(3) for unknown in range(3)])

def accumulation_terms(state, pore_volume, old_mass):

    def inner(press, water, gas):
        oil = 1.0 - water - gas
        rock = pore_volume * (1.0 + compress_rock * press)
        oil_density = 1.0 + compress_oil * press
        solved = solution_base + solution_slope * press
        water_term = (rock * water * (1.0 + compress_water * press) - old_mass[0]) / time_step
        oil_term = (rock * oil * oil_density - old_mass[1]) / time_step
        gas_term = (rock * (gas * (1.0 + compress_gas * press) + solved * oil * oil_density) - old_mass[2]) / time_step
        return (water_term, oil_term, gas_term)
    values, pullback = jax.vjp(inner, *state)
    block = pick_block(unit_rows(values, pullback), 0)
    return (jnp.stack(values), block, block[0] + block[3] + block[6])

def flux_terms(near, far, depth_near, depth_far, transmit):

    def inner(press_near, water_near, gas_near, press_far, water_far, gas_far):
        movers_near = mobilities(press_near, water_near, gas_near)
        movers_far = mobilities(press_far, water_far, gas_far)
        half = 0.5 * transmit
        drop = press_near - press_far
        rise = depth_near - depth_far
        oil_drive = drop - gravity_oil * rise
        water_flux = half * (movers_near[0] + movers_far[0]) * (drop - gravity_water * rise)
        oil_flux = half * (movers_near[1] + movers_far[1]) * oil_drive
        gas_flux = half * ((movers_near[2] + movers_far[2]) * (drop - gravity_gas * rise) + (movers_near[3] + movers_far[3]) * oil_drive)
        conduct = half * (movers_near[4] + movers_far[4])
        return ((water_flux, oil_flux, gas_flux), conduct)
    values, pullback, conduct = jax.vjp(inner, *near, *far, has_aux=True)
    rows = unit_rows(values, pullback)
    return (jnp.stack(values), pick_block(rows, 0), pick_block(rows, 3), conduct)

def well_terms(state, well_index, well_pressure):

    def inner(press, water, gas):
        movers = mobilities(press, water, gas)
        drive = well_index * (well_pressure - press)
        return ((drive * movers[0], drive * movers[1], drive * (movers[2] + movers[3])), well_index * movers[4])
    values, pullback, reach = jax.vjp(inner, *state, has_aux=True)
    return (jnp.stack(values), pick_block(unit_rows(values, pullback), 0), reach)

def leading(values, axis):
    return lax.slice_in_dim(values, 0, values.shape[axis] - 1, axis=axis)

def trailing(values, axis):
    return lax.slice_in_dim(values, 1, values.shape[axis], axis=axis)

def pad_faces(values, axis):
    widths = [(0, 0)] * values.ndim
    widths[axis] = (1, 1)
    return jnp.pad(values, widths)

def direction_terms(state, depth, transmit, axis):
    flows, left_block, right_block, conduct = flux_terms(tuple((leading(field, axis) for field in state)), tuple((trailing(field, axis) for field in state)), leading(depth, axis), trailing(depth, axis), leading(transmit, axis))
    return (pad_faces(flows, axis + 1), pad_faces(left_block, axis + 1), pad_faces(right_block, axis + 1), pad_faces(conduct, axis))

def add_faces(totals, face_values, axis):
    residual, diagonal, pressure_diagonal = totals
    flows, left_block, right_block, conduct = face_values
    residual = residual + trailing(flows, axis + 1) - leading(flows, axis + 1)
    diagonal = diagonal + trailing(left_block, axis + 1) - leading(right_block, axis + 1)
    pressure_diagonal = pressure_diagonal + trailing(conduct, axis) + leading(conduct, axis)
    blocks = jnp.stack([trailing(right_block, axis + 1), -trailing(left_block, axis + 1)])
    return ((residual, diagonal, pressure_diagonal), blocks)

def neighbour_sum(conduct, padded, axis):
    upper = lax.slice_in_dim(padded, 2, padded.shape[axis], axis=axis)
    lower = lax.slice_in_dim(padded, 0, padded.shape[axis] - 2, axis=axis)
    return trailing(conduct, axis) * upper + leading(conduct, axis) * lower

def to_blocks(values):
    lead = values.shape[:-3]
    count = len(lead)
    shaped = values.reshape(lead + (GI, CI, GJ, CJ, NZ))
    shaped = jnp.swapaxes(shaped, count + 1, count + 2)
    return shaped.reshape(lead + (OWNERS * CELLS,))

def from_blocks(values):
    lead = values.shape[:-1]
    count = len(lead)
    shaped = values.reshape(lead + (GI, GJ, CI, CJ, NZ))
    shaped = jnp.swapaxes(shaped, count + 1, count + 2)
    return shaped.reshape(lead + (NI, NJ, NZ))

def partner_view(values):
    padded = jnp.pad(values, ((1, 1), (1, 1), (0, 0), (0, 0), (0, 0)))
    lines = []
    for first_offset in range(3):
        entries = []
        for second_offset in range(3):
            entries.append(padded[first_offset:first_offset + GI, second_offset:second_offset + GJ, 2 - first_offset, 2 - second_offset])
        lines.append(jnp.stack(entries, axis=2))
    return jnp.stack(lines, axis=2)

def reference(pressure, water_sat, gas_sat, depth, pore_volume, old_mass, transmissibility, fault_column, fault_layer, fault_transmissibility, perforation_cell, well_index, well_pressure):
    state = (pressure, water_sat, gas_sat)
    residual, diagonal, pressure_diagonal = accumulation_terms(state, pore_volume, old_mass)
    totals = (residual, diagonal, pressure_diagonal)
    conducts = []
    faces = []
    for axis in range(3):
        terms = direction_terms(state, depth, transmissibility[axis], axis)
        totals, blocks = add_faces(totals, terms, axis)
        conducts.append(terms[3])
        faces.append(blocks)
    face_blocks = jnp.stack(faces).astype(jnp.bfloat16)
    residual, diagonal, pressure_diagonal = totals
    flat_state = to_blocks(jnp.stack([pressure, water_sat, gas_sat, depth]))
    residual = to_blocks(residual)
    diagonal = to_blocks(diagonal)
    pressure_diagonal = to_blocks(pressure_diagonal)
    column_grid = fault_column.reshape(GI, GJ, 3, 3, SLOTS)
    layer_grid = fault_layer.reshape(GI, GJ, 3, 3, SLOTS)
    far_column = partner_view(column_grid)
    far_layer = partner_view(layer_grid)
    block_i = lax.broadcasted_iota(jnp.int32, (GI, GJ, 3, 3, 1), 0)
    block_j = lax.broadcasted_iota(jnp.int32, (GI, GJ, 3, 3, 1), 1)
    offset_i = lax.broadcasted_iota(jnp.int32, (GI, GJ, 3, 3, 1), 2) - 1
    offset_j = lax.broadcasted_iota(jnp.int32, (GI, GJ, 3, 3, 1), 3) - 1
    partner = jnp.clip(block_i + offset_i, 0, GI - 1) * GJ + jnp.clip(block_j + offset_j, 0, GJ - 1)
    own_all = ((block_i * GJ + block_j) * CELLS + column_grid * NZ + layer_grid).reshape(-1).astype(jnp.int32)
    far_all = (partner * CELLS + far_column * NZ + far_layer).reshape(-1).astype(jnp.int32)
    near_state = jnp.take(flat_state, own_all, axis=1).reshape(4, OWNERS, 3, 3, SLOTS)
    far_state = jnp.take(flat_state, far_all, axis=1).reshape(4, OWNERS, 3, 3, SLOTS)
    flows, left_block, right_block, fault_conduct = flux_terms((near_state[0], near_state[1], near_state[2]), (far_state[0], far_state[1], far_state[2]), near_state[3], far_state[3], fault_transmissibility)
    residual = residual.at[:, own_all].add(flows.reshape(3, -1))
    diagonal = diagonal.at[:, own_all].add(left_block.reshape(9, -1))
    pressure_diagonal = pressure_diagonal.at[own_all].add(fault_conduct.reshape(-1))
    fault_blocks = right_block.astype(jnp.bfloat16)
    owner_ids = jnp.arange(OWNERS, dtype=jnp.int32)
    perforated = (owner_ids[:, None] * CELLS + perforation_cell).reshape(-1)
    perf_state = tuple((jnp.take(flat_state[field], perforated) for field in range(3)))
    rates, rate_block, reach = well_terms(perf_state, well_index.reshape(-1), well_pressure.reshape(-1))
    residual = residual.at[:, perforated].add(-rates)
    diagonal = diagonal.at[:, perforated].add(-rate_block)
    pressure_diagonal = pressure_diagonal.at[perforated].add(reach)
    right_side = -(residual[0] + residual[1] + residual[2])
    first = right_side / pressure_diagonal
    first_grid = from_blocks(first)
    gathered = jnp.zeros((NI, NJ, NZ), jnp.float32)
    for axis in range(3):
        gathered = gathered + neighbour_sum(conducts[axis], pad_faces(first_grid, axis), axis)
    gathered = to_blocks(gathered)
    gathered = gathered.at[own_all].add(fault_conduct.reshape(-1) * jnp.take(first, far_all))
    update = (right_side + gathered) / pressure_diagonal
    return (from_blocks(residual), from_blocks(diagonal).astype(jnp.bfloat16), face_blocks, fault_blocks, from_blocks(update))
```

```python
import jax
import jax.numpy as jnp
from jax import lax
from jax.experimental import pallas as pl
from jax.experimental.pallas import tpu as pltpu
from jax.sharding import PartitionSpec as P

F32 = jnp.float32
BF16 = jnp.bfloat16
MESH = pl.DeviceIdType.MESH
CHUNK = 256
VMEM_BYTES = 48 * 1024 * 1024


def split(x):
    hi = x.astype(BF16)
    return hi, (x - hi.astype(F32)).astype(BF16)


def cell_terms(p, sw, sg):
    oil = 1.0 - sw - sg
    bw = 1.0 + 0.05 * p
    bo = 1.0 + 0.1 * p
    bg = 1.0 + 0.4 * p
    rs = 0.5 + 0.2 * p
    w2 = sw * (sw * (1.0 / 0.3))
    o2 = oil * (oil * (1.0 / 0.8))
    g2 = sg * (sg * (1.0 / 0.05))
    mo = bo * o2
    mo_p = 0.1 * o2
    mo_o = bo * (oil * (2.0 / 0.8))
    return dict(
        mw=bw * w2,
        mo=mo,
        mg=bg * g2,
        md=rs * mo,
        mw_p=0.05 * w2,
        mw_s=bw * (sw * (2.0 / 0.3)),
        mo_p=mo_p,
        mo_o=mo_o,
        mg_p=0.4 * g2,
        mg_s=bg * (sg * (2.0 / 0.05)),
        md_p=0.2 * mo + rs * mo_p,
        md_o=rs * mo_o,
    )


def face_terms(t, a, b, pa, pb, za, zb):
    half = 0.5 * t
    hp = half * (pa - pb)
    hz = half * (za - zb)
    ww = hp - 0.1 * hz
    wo = hp - 0.08 * hz
    wg = hp - 0.02 * hz
    sum_w = a["mw"] + b["mw"]
    sum_o = a["mo"] + b["mo"]
    sum_g = a["mg"] + b["mg"]
    sum_d = a["md"] + b["md"]
    mw = half * sum_w
    mo = half * sum_o
    mgd = half * (sum_g + sum_d)
    flux = (sum_w * ww, sum_o * wo, sum_g * wg + sum_d * wo)
    return (hp, hz, mw, mo, mgd) + flux, (ww, wo, wg)


def block_rows(c, ww, wo, wg, mw, mo, mgd):
    oil = c["mo_o"] * wo
    solved = c["md_o"] * wo
    zero = jnp.zeros_like(ww)
    return (
        c["mw_p"] * ww + mw,
        c["mw_s"] * ww,
        zero,
        c["mo_p"] * wo + mo,
        -oil,
        -oil,
        c["mg_p"] * wg + c["md_p"] * wo + mgd,
        -solved,
        c["mg_s"] * wg - solved,
    )


def neighbour(d):
    a, b = lax.axis_index("col"), lax.axis_index("row")
    ta, tb = a + d // 3 - 1, b + d % 3 - 1
    na, nb = lax.axis_size("col"), lax.axis_size("row")
    there = (ta >= 0) & (ta < na) & (tb >= 0) & (tb < nb)
    return there, (ta, tb)


def eight(body):
    def step(e, carry):
        body(jnp.where(e >= 4, e + 1, e))
        return carry

    lax.fori_loop(0, 8, step, 0)


SIDES = (7, 1, 5, 3)


def greet():
    barrier = pltpu.get_barrier_semaphore()
    count = 0
    for d in (0, 1, 2, 3, 5, 6, 7, 8):
        there, target = neighbour(d)

        @pl.when(there)
        def _():
            pl.semaphore_signal(barrier, inc=1, device_id=target, device_id_type=MESH)

        count = count + there.astype(jnp.int32)
    return barrier, count


def halo_copy(src, dst, k, count, send_sem, recv_sem):
    return pltpu.make_async_remote_copy(
        src_ref=src.at[k, pl.ds(0, count)],
        dst_ref=dst.at[k, pl.ds(0, count)],
        send_sem=send_sem.at[k],
        recv_sem=recv_sem.at[k],
        device_id=neighbour(SIDES[k])[1],
        device_id_type=MESH,
    )


def fault_copy(src, dst, d, send_sem, recv_sem, back):
    return pltpu.make_async_remote_copy(
        src_ref=src.at[d],
        dst_ref=dst.at[back],
        send_sem=send_sem.at[d],
        recv_sem=recv_sem.at[back],
        device_id=neighbour(d)[1],
        device_id_type=MESH,
    )


def wait_halos(src, dst, counts, send_sem, recv_sem):
    for k in range(4):
        copy = halo_copy(src, dst, k, counts[k], send_sem, recv_sem)
        pl.when(neighbour(SIDES[k])[0])(copy.wait_send)
        pl.when(neighbour(8 - SIDES[k])[0])(copy.wait_recv)


def wait_faults(src, dst, send_sem, recv_sem):
    def one(d):
        copy = fault_copy(src, dst, d, send_sem, recv_sem, d)

        @pl.when(neighbour(d)[0])
        def _():
            copy.wait_send()
            copy.wait_recv()

    eight(one)


def cell_rows(column, layer):
    return (column >> 4) * 8 + (column & 7), ((column >> 3) & 1) * 128 + layer


def hot(index, size):
    slots = index.shape[1]
    row = jnp.broadcast_to(index.astype(F32), (16, slots)).astype(BF16)
    iota = lax.broadcasted_iota(jnp.int32, (size, slots), 0).astype(F32).astype(BF16)
    return iota.reshape(size // 16, 16, slots) == row[None]


def hot_values(mask, value_row):
    slots = value_row.shape[1]
    hi, lo = split(jnp.broadcast_to(value_row, (16, slots)))
    zero = jnp.zeros((), BF16)
    return [jnp.where(mask, v[None], zero).reshape(128, slots) for v in (hi, lo)]


def hot_ones(mask):
    size = mask.shape[0] * 16
    return jnp.where(mask, jnp.ones((), BF16), jnp.zeros((), BF16)).reshape(size, mask.shape[2])


def as_rows(x):
    low = x[:, 0:8, :].reshape(128, 128)
    high = x[:, 8:16, :].reshape(128, 128)
    return jnp.concatenate([low, high], axis=1)


def exchange_kernel(
    p_ref, sw_ref, sg_ref, z_ref, t_ref, fc_ref, fl_ref,
    near_ref, far_ref, halo_ref,
    sbuf, rbuf, hsend, hrecv, ghi, glo, fs, fr, hs, hr,
):
    barrier, count = greet()
    fields = (p_ref, sw_ref, sg_ref, z_ref)
    for f, ref in enumerate(fields):
        hsend[0, f] = ref[15]
        hsend[1, f] = ref[0]
        hsend[2, f] = ref[:, 15, :]
        hsend[3, f] = ref[:, 0, :]
    hsend[0, 4] = t_ref[0, 15]
    hsend[2, 4] = t_ref[1, :, 15, :]
    counts = (5, 4, 5, 4)
    for k in range(4):
        there = neighbour(8 - SIDES[k])[0]

        @pl.when(jnp.logical_not(there))
        def _():
            hrecv[k] = jnp.zeros_like(hrecv[k])

    sbuf[4] = jnp.zeros_like(sbuf[4])
    rbuf[4] = jnp.zeros_like(rbuf[4])

    def clear(d):
        @pl.when(jnp.logical_not(neighbour(d)[0]))
        def _():
            rbuf[d] = jnp.zeros_like(rbuf[d])

    eight(clear)
    pl.semaphore_wait(barrier, count)
    for k in range(4):
        pl.when(neighbour(SIDES[k])[0])(halo_copy(hsend, hrecv, k, counts[k], hs, hr).start)
    for f, ref in enumerate(fields):
        hi, lo = split(as_rows(ref[...]))
        ghi[pl.ds(f * 128, 128), :] = hi
        glo[pl.ds(f * 128, 128), :] = lo

    def gather(d):
        di, dj = d // 3, d % 3
        for c in range(0, sbuf.shape[2], CHUNK):
            column = fc_ref[0, di, pl.ds(dj, 1), pl.ds(c, CHUNK)]
            layer = fl_ref[0, di, pl.ds(dj, 1), pl.ds(c, CHUNK)]
            row, lane = cell_rows(column, layer)
            pick = hot_ones(hot(lane, 256))
            lines = jnp.dot(ghi[...], pick, preferred_element_type=F32)
            lines = lines + jnp.dot(glo[...], pick, preferred_element_type=F32)
            mask = lax.broadcasted_iota(jnp.int32, (128, CHUNK), 0) == row
            for f in range(4):
                part = lines[f * 128 : (f + 1) * 128]
                sbuf[d, pl.ds(f, 1), pl.ds(c, CHUNK)] = jnp.sum(
                    jnp.where(mask, part, 0.0), axis=0, keepdims=True
                )
        pl.when(neighbour(d)[0])(fault_copy(sbuf, rbuf, d, fs, fr, 8 - d).start)

    eight(gather)
    wait_halos(hsend, hrecv, counts, hs, hr)
    for k in (0, 2):
        halo_ref[k] = hrecv[k]
        halo_ref[k + 1, 0:4] = hrecv[k + 1, 0:4]
        own = hsend[k, 4]
        halo_ref[k + 1, 4] = jnp.where(neighbour(SIDES[k])[0], own, jnp.zeros_like(own))
    wait_faults(sbuf, rbuf, fs, fr)
    for d in range(9):
        for f in range(4):
            near_ref[f, d // 3, pl.ds(d % 3, 1), :] = sbuf[d, pl.ds(f, 1), :]
            far_ref[f, d // 3, pl.ds(d % 3, 1), :] = rbuf[d, pl.ds(f, 1), :]


def terms_kernel(
    p_ref, sw_ref, sg_ref, z_ref, pv_ref, om_ref, t_ref, fc_ref, fl_ref, ft_ref,
    pc_ref, wi_ref, wp_ref, near_ref, far_ref, halo_ref,
    res_ref, diag_ref, face_ref, fault_ref, first_ref, rhs_ref, pd_ref, cond_ref, condlow_ref, fcond_ref,
    blocks, acc, wacc, lowj, chan, out_sem,
):
    slots = fc_ref.shape[3]

    def low_face(k, fields):
        a = [halo_ref[k, f] for f in range(4)]
        values, _ = face_terms(
            halo_ref[k, 4], cell_terms(*a[:3]), cell_terms(*fields[:3]), a[0], fields[0], a[3], fields[3]
        )
        condlow_ref[k // 2] = values[2] + values[3] + values[4]
        return lower_side(values)

    def lower_side(values):
        return (-values[0], -values[1], values[2], values[3], values[4]) + tuple(-v for v in values[5:])

    for v, value in enumerate(low_face(2, [r[:, 0, :] for r in (p_ref, sw_ref, sg_ref, z_ref)])):
        lowj[v] = value
    carry = low_face(0, [r[0] for r in (p_ref, sw_ref, sg_ref, z_ref)])

    row_id = lax.broadcasted_iota(jnp.int32, (16, 128), 0)
    lane_id = lax.broadcasted_iota(jnp.int32, (16, 128), 1)

    def plane(i, carry):
        refs = (p_ref, sw_ref, sg_ref, z_ref)
        own = [r[i] for r in refs]
        a = cell_terms(*own[:3])
        last = i == 15
        after = jnp.minimum(i + 1, 15)
        total = list(carry)
        out_carry = None
        for n in range(3):
            if n == 0:
                nxt = [jnp.where(last, halo_ref[1, f], r[after]) for f, r in enumerate(refs)]
                t = jnp.where(last, halo_ref[1, 4], t_ref[0, i])
            elif n == 1:
                nxt = [
                    jnp.where(row_id == 15, halo_ref[3, f, pl.ds(i, 1), :], pltpu.roll(own[f], 15, 0))
                    for f in range(4)
                ]
                t = jnp.where(row_id == 15, halo_ref[3, 4, pl.ds(i, 1), :], t_ref[1, i])
            else:
                nxt = [pltpu.roll(own[f], 127, 1) for f in range(4)]
                t = jnp.where(lane_id == 127, 0.0, t_ref[2, i])
            b = cell_terms(*nxt[:3])
            values, (ww, wo, wg) = face_terms(t, a, b, own[0], nxt[0], own[3], nxt[3])
            mw, mo, mgd = values[2:5]
            cond_ref[n, i] = mw + mo + mgd
            upper = block_rows(b, ww, wo, wg, -mw, -mo, -mgd)
            lower = block_rows(a, -ww, -wo, -wg, -mw, -mo, -mgd)
            for e in range(9):
                blocks[n, 0, e, i] = upper[e].astype(BF16)
                blocks[n, 1, e, i] = lower[e].astype(BF16)
            total = [x + y for x, y in zip(total, values)]
            below = lower_side(values)
            if n == 0:
                out_carry = below
            elif n == 1:
                for v in range(8):
                    shifted = jnp.where(row_id == 0, lowj[v, pl.ds(i, 1), :], pltpu.roll(below[v], 1, 0))
                    total[v] = total[v] + shifted
            else:
                total = [x + pltpu.roll(y, 1, 1) for x, y in zip(total, below)]
        for v in range(8):
            at = pl.multiple_of(v * 128 + i * 8, 8)
            acc[pl.ds(at, 8), 0:128] = total[v][0:8]
            acc[pl.ds(at, 8), 128:256] = total[v][8:16]
        return tuple(out_carry)

    lax.fori_loop(0, 16, plane, tuple(carry))
    out_copy = pltpu.make_async_copy(blocks, face_ref, out_sem)
    out_copy.start()

    near = [near_ref[f] for f in range(4)]
    far = [far_ref[f] for f in range(4)]
    a, b = cell_terms(*near[:3]), cell_terms(*far[:3])
    values, (ww, wo, wg) = face_terms(ft_ref[0], a, b, near[0], far[0], near[3], far[3])
    mw, mo, mgd = values[2:5]
    fcond_ref[...] = mw + mo + mgd
    for v in range(8):
        chan[v] = values[v]
    for e, value in enumerate(block_rows(b, ww, wo, wg, -mw, -mo, -mgd)):
        fault_ref[e, 0] = value.astype(BF16)

    def scatter(d):
        di, dj = d // 3, d % 3
        for c in range(0, slots, CHUNK):
            column = fc_ref[0, di, pl.ds(dj, 1), pl.ds(c, CHUNK)]
            layer = fl_ref[0, di, pl.ds(dj, 1), pl.ds(c, CHUNK)]
            row, lane = cell_rows(column, layer)
            put = hot_ones(hot(lane, 256))
            mask = hot(row, 128)
            his, los = [], []
            for v in range(8):
                hi, lo = hot_values(mask, chan[v, di, pl.ds(dj, 1), pl.ds(c, CHUNK)])
                his.append(hi)
                los.append(lo)
            weighted = jnp.concatenate(
                [jnp.concatenate(his, axis=0), jnp.concatenate(los, axis=0)], axis=1
            )
            acc[...] += lax.dot_general(
                weighted,
                jnp.concatenate([put, put], axis=1),
                (((1,), (1,)), ((), ())),
                preferred_element_type=F32,
            )

    eight(scatter)

    cell = pc_ref[...]
    row, lane = cell_rows(cell >> 7, cell & 127)
    mask = hot(row, 128)
    hi_w, lo_w = hot_values(mask, wi_ref[...])
    hi_q, lo_q = hot_values(mask, wi_ref[...] * wp_ref[...])
    weighted = jnp.concatenate(
        [jnp.concatenate([hi_w, hi_q], axis=0), jnp.concatenate([lo_w, lo_q], axis=0)], axis=1
    )
    put = hot_ones(hot(lane, 256))
    wacc[...] = lax.dot_general(
        weighted,
        jnp.concatenate([put, put], axis=1),
        (((1,), (1,)), ((), ())),
        preferred_element_type=F32,
    )

    def rows_of(ref, start):
        at = pl.multiple_of(start, 8)
        return jnp.concatenate([ref[pl.ds(at, 8), 0:128], ref[pl.ds(at, 8), 128:256]], axis=0)

    def finish(i, carry):
        p, sw, sg = p_ref[i], sw_ref[i], sg_ref[i]
        c = cell_terms(p, sw, sg)
        hp, hz, mw, mo, mgd, rw, ro, rg = [rows_of(acc, v * 128 + i * 8) for v in range(8)]
        well = rows_of(wacc, i * 8)
        drive = rows_of(wacc, 128 + i * 8) - p * well
        oil = 1.0 - sw - sg
        pv = pv_ref[i]
        rock = 2.0 * (pv * (1.0 + 0.02 * p))
        rock_p = 0.04 * pv
        bw, bo, bg, rs = 1.0 + 0.05 * p, 1.0 + 0.1 * p, 1.0 + 0.4 * p, 0.5 + 0.2 * p
        ob = oil * bo
        gas = sg * bg + rs * ob
        r0 = rock * sw * bw - 2.0 * om_ref[0, i] + rw - drive * c["mw"]
        r1 = rock * ob - 2.0 * om_ref[1, i] + ro - drive * c["mo"]
        r2 = rock * gas - 2.0 * om_ref[2, i] + rg - drive * (c["mg"] + c["md"])
        res_ref[0, i], res_ref[1, i], res_ref[2, i] = r0, r1, r2
        a0 = rock_p * sw * bw + rock * sw * 0.05
        a3 = rock_p * ob + rock * oil * 0.1
        a6 = rock_p * gas + rock * (0.4 * sg + 0.2 * ob + 0.1 * rs * oil)
        total = c["mw"] + c["mo"] + c["mg"] + c["md"]
        pd = a0 + a3 + a6 + mw + mo + mgd + well * total
        dw = hp - 0.1 * hz - drive
        do = hp - 0.08 * hz - drive
        dg = hp - 0.02 * hz - drive
        solved = c["md_o"] * do
        pair = -(rock * bo) - c["mo_o"] * do
        gas_water = -(rock * rs * bo) - solved
        rows = (
            a0 + c["mw_p"] * dw + mw + well * c["mw"],
            rock * bw + c["mw_s"] * dw,
            jnp.zeros_like(p),
            a3 + c["mo_p"] * do + mo + well * c["mo"],
            pair,
            pair,
            a6 + c["mg_p"] * dg + c["md_p"] * do + mgd + well * (c["mg"] + c["md"]),
            gas_water,
            rock * bg + c["mg_s"] * dg + gas_water,
        )
        for e in range(9):
            diag_ref[e, i] = rows[e].astype(BF16)
        rhs = -(r0 + r1 + r2)
        rhs_ref[i] = rhs
        pd_ref[i] = pd
        first_ref[i] = rhs / pd
        return carry

    lax.fori_loop(0, 16, finish, 0)
    out_copy.wait()


def update_kernel(
    first_ref, rhs_ref, pd_ref, cond_ref, condlow_ref, fcond_ref, fc_ref, fl_ref,
    out_ref,
    sbuf, rbuf, hsend, hrecv, ghl, acc, fs, fr, hs, hr,
):
    slots = fc_ref.shape[3]
    barrier, count = greet()
    hsend[0, 0] = first_ref[15]
    hsend[1, 0] = first_ref[0]
    hsend[2, 0] = first_ref[:, 15, :]
    hsend[3, 0] = first_ref[:, 0, :]
    counts = (1, 1, 1, 1)
    for k in range(4):
        there = neighbour(8 - SIDES[k])[0]

        @pl.when(jnp.logical_not(there))
        def _():
            hrecv[k] = jnp.zeros_like(hrecv[k])

    def clear(d):
        @pl.when(jnp.logical_not(neighbour(d)[0]))
        def _():
            rbuf[d] = jnp.zeros_like(rbuf[d])

    eight(clear)
    hi, lo = split(as_rows(first_ref[...]))
    ghl[0:128, :] = hi
    ghl[128:256, :] = lo
    pl.semaphore_wait(barrier, count)
    for k in range(4):
        pl.when(neighbour(SIDES[k])[0])(halo_copy(hsend, hrecv, k, 1, hs, hr).start)

    def gather(d):
        di, dj = d // 3, d % 3
        for c in range(0, slots, CHUNK):
            column = fc_ref[0, di, pl.ds(dj, 1), pl.ds(c, CHUNK)]
            layer = fl_ref[0, di, pl.ds(dj, 1), pl.ds(c, CHUNK)]
            row, lane = cell_rows(column, layer)
            lines = jnp.dot(ghl[...], hot_ones(hot(lane, 256)), preferred_element_type=F32)
            mask = lax.broadcasted_iota(jnp.int32, (128, CHUNK), 0) == row
            sbuf[d, :, pl.ds(c, CHUNK)] = jnp.sum(
                jnp.where(mask, lines[0:128] + lines[128:256], 0.0), axis=0, keepdims=True
            )
        pl.when(neighbour(d)[0])(fault_copy(sbuf, rbuf, d, fs, fr, 8 - d).start)

    eight(gather)
    acc[...] = jnp.zeros_like(acc)
    wait_halos(hsend, hrecv, counts, hs, hr)
    wait_faults(sbuf, rbuf, fs, fr)

    def scatter(d):
        di, dj = d // 3, d % 3
        for c in range(0, slots, CHUNK):
            column = fc_ref[0, di, pl.ds(dj, 1), pl.ds(c, CHUNK)]
            layer = fl_ref[0, di, pl.ds(dj, 1), pl.ds(c, CHUNK)]
            row, lane = cell_rows(column, layer)
            value = fcond_ref[di, pl.ds(dj, 1), pl.ds(c, CHUNK)] * rbuf[d, :, pl.ds(c, CHUNK)]
            acc[...] += lax.dot_general(
                jnp.concatenate(hot_values(hot(row, 128), value), axis=0),
                hot_ones(hot(lane, 256)),
                (((1,), (1,)), ((), ())),
                preferred_element_type=F32,
            )

    eight(scatter)
    row_id = lax.broadcasted_iota(jnp.int32, (16, 128), 0)

    def finish(i, carry):
        own = first_ref[i]
        before, after = jnp.maximum(i - 1, 0), jnp.minimum(i + 1, 15)
        up = jnp.where(i == 15, hrecv[1, 0], first_ref[after])
        down = jnp.where(i == 0, hrecv[0, 0], first_ref[before])
        total = cond_ref[0, i] * up
        total += jnp.where(i == 0, condlow_ref[0], cond_ref[0, before]) * down
        cj = cond_ref[1, i]
        up = jnp.where(row_id == 15, hrecv[3, 0, pl.ds(i, 1), :], pltpu.roll(own, 15, 0))
        down = jnp.where(row_id == 0, hrecv[2, 0, pl.ds(i, 1), :], pltpu.roll(own, 1, 0))
        cj_low = jnp.where(row_id == 0, condlow_ref[1, pl.ds(i, 1), :], pltpu.roll(cj, 1, 0))
        total += cj * up + cj_low * down
        ck = cond_ref[2, i]
        total += ck * pltpu.roll(own, 127, 1) + pltpu.roll(ck * own, 1, 1)
        at = pl.multiple_of(i * 8, 8)
        fault = acc[pl.ds(at, 8), :] + acc[pl.ds(at + 128, 8), :]
        total += jnp.concatenate([fault[:, 0:128], fault[:, 128:256]], axis=0)
        out_ref[i] = (rhs_ref[i] + total) / pd_ref[i]
        return carry

    lax.fori_loop(0, 16, finish, 0)


def vmem(count):
    return [pl.BlockSpec(memory_space=pltpu.VMEM)] * count


def per_device(p, sw, sg, z, pv, om, t, fc, fl, ft, pc, wi, wp):
    slots = fc.shape[3]
    block = jax.ShapeDtypeStruct(p.shape, F32)
    dma = pltpu.SemaphoreType.DMA
    near, far, halo = pl.pallas_call(
        exchange_kernel,
        out_shape=[
            jax.ShapeDtypeStruct((4, 3, 3, slots), F32),
            jax.ShapeDtypeStruct((4, 3, 3, slots), F32),
            jax.ShapeDtypeStruct((4, 5, 16, 128), F32),
        ],
        in_specs=vmem(7),
        out_specs=vmem(3),
        scratch_shapes=[
            pltpu.VMEM((9, 4, slots), F32),
            pltpu.VMEM((9, 4, slots), F32),
            pltpu.VMEM((4, 5, 16, 128), F32),
            pltpu.VMEM((4, 5, 16, 128), F32),
            pltpu.VMEM((512, 256), BF16),
            pltpu.VMEM((512, 256), BF16),
            dma((9,)),
            dma((9,)),
            dma((4,)),
            dma((4,)),
        ],
        compiler_params=pltpu.CompilerParams(
            collective_id=0, has_side_effects=True, vmem_limit_bytes=VMEM_BYTES
        ),
        name="exchange",
    )(p, sw, sg, z, t, fc, fl)
    res, diag, face, fault, first, rhs, pd, cond, condlow, fcond = pl.pallas_call(
        terms_kernel,
        out_shape=[
            jax.ShapeDtypeStruct((3, 16, 16, 128), F32),
            jax.ShapeDtypeStruct((9, 16, 16, 128), BF16),
            jax.ShapeDtypeStruct((3, 2, 9, 16, 16, 128), BF16),
            jax.ShapeDtypeStruct((9, 1, 3, 3, slots), BF16),
            block,
            block,
            block,
            jax.ShapeDtypeStruct((3, 16, 16, 128), F32),
            jax.ShapeDtypeStruct((2, 16, 128), F32),
            jax.ShapeDtypeStruct((3, 3, slots), F32),
        ],
        in_specs=vmem(16),
        out_specs=vmem(2) + [pl.BlockSpec(memory_space=pl.ANY)] + vmem(7),
        scratch_shapes=[
            pltpu.VMEM((3, 2, 9, 16, 16, 128), BF16),
            pltpu.VMEM((1024, 256), F32),
            pltpu.VMEM((256, 256), F32),
            pltpu.VMEM((8, 16, 128), F32),
            pltpu.VMEM((8, 3, 3, slots), F32),
            dma,
        ],
        compiler_params=pltpu.CompilerParams(vmem_limit_bytes=VMEM_BYTES),
        name="terms",
    )(p, sw, sg, z, pv, om, t, fc, fl, ft, pc, wi, wp, near, far, halo)
    update = pl.pallas_call(
        update_kernel,
        out_shape=block,
        in_specs=vmem(8),
        out_specs=vmem(1)[0],
        scratch_shapes=[
            pltpu.VMEM((9, 1, slots), F32),
            pltpu.VMEM((9, 1, slots), F32),
            pltpu.VMEM((4, 1, 16, 128), F32),
            pltpu.VMEM((4, 1, 16, 128), F32),
            pltpu.VMEM((256, 256), BF16),
            pltpu.VMEM((256, 256), F32),
            dma((9,)),
            dma((9,)),
            dma((4,)),
            dma((4,)),
        ],
        compiler_params=pltpu.CompilerParams(
            collective_id=1, has_side_effects=True, vmem_limit_bytes=VMEM_BYTES
        ),
        name="update",
    )(first, rhs, pd, cond, condlow, fcond, fc, fl)
    return res, diag, face, fault, update


def solution(mesh):
    cells = P("col", "row", None)
    stacked = P(None, "col", "row", None)
    owned = P(("col", "row"), None, None, None)
    wells = P(("col", "row"), None)
    return jax.shard_map(
        per_device,
        mesh=mesh,
        in_specs=(cells,) * 5 + (stacked,) * 2 + (owned,) * 3 + (wells,) * 3,
        out_specs=(
            stacked,
            stacked,
            P(None, None, None, "col", "row", None),
            P(None, ("col", "row"), None, None, None),
            cells,
        ),
        check_vma=False,
    )
```

```python
import jax
import jax.numpy as jnp
from jax import lax
from jax.experimental import pallas as pl
from jax.experimental.pallas import tpu as pltpu
from jax.sharding import PartitionSpec as P

F32 = jnp.float32
BF16 = jnp.bfloat16
MESH = pl.DeviceIdType.MESH
VMEM_BYTES = 40 * 1024 * 1024


def split(x):
    hi = x.astype(BF16)
    return hi, (x - hi.astype(F32)).astype(BF16)


def cell_terms(p, sw, sg):
    oil = 1.0 - sw - sg
    bw = 1.0 + 0.05 * p
    bo = 1.0 + 0.1 * p
    bg = 1.0 + 0.4 * p
    rs = 0.5 + 0.2 * p
    w2 = sw * (sw * (1.0 / 0.3))
    o2 = oil * (oil * (1.0 / 0.8))
    g2 = sg * (sg * (1.0 / 0.05))
    mo = bo * o2
    mo_p = 0.1 * o2
    mo_o = bo * (oil * (2.0 / 0.8))
    return dict(
        mw=bw * w2,
        mo=mo,
        mg=bg * g2,
        md=rs * mo,
        mw_p=0.05 * w2,
        mw_s=bw * (sw * (2.0 / 0.3)),
        mo_p=mo_p,
        mo_o=mo_o,
        mg_p=0.4 * g2,
        mg_s=bg * (sg * (2.0 / 0.05)),
        md_p=0.2 * mo + rs * mo_p,
        md_o=rs * mo_o,
    )


def face_terms(t, a, b, pa, pb, za, zb):
    half = 0.5 * t
    hp = half * (pa - pb)
    hz = half * (za - zb)
    ww = hp - 0.1 * hz
    wo = hp - 0.08 * hz
    wg = hp - 0.02 * hz
    sum_w = a["mw"] + b["mw"]
    sum_o = a["mo"] + b["mo"]
    sum_g = a["mg"] + b["mg"]
    sum_d = a["md"] + b["md"]
    mw = half * sum_w
    mo = half * sum_o
    mgd = half * (sum_g + sum_d)
    flux = (sum_w * ww, sum_o * wo, sum_g * wg + sum_d * wo)
    return (hp, hz, mw, mo, mgd) + flux, (ww, wo, wg)


def block_rows(c, ww, wo, wg, mw, mo, mgd):
    oil = c["mo_o"] * wo
    solved = c["md_o"] * wo
    zero = jnp.zeros_like(ww)
    return (
        c["mw_p"] * ww + mw,
        c["mw_s"] * ww,
        zero,
        c["mo_p"] * wo + mo,
        -oil,
        -oil,
        c["mg_p"] * wg + c["md_p"] * wo + mgd,
        -solved,
        c["mg_s"] * wg - solved,
    )


def neighbour(d):
    a, b = lax.axis_index("col"), lax.axis_index("row")
    ta, tb = a + d // 3 - 1, b + d % 3 - 1
    na, nb = lax.axis_size("col"), lax.axis_size("row")
    there = (ta >= 0) & (ta < na) & (tb >= 0) & (tb < nb)
    return there, (ta, tb)


def group(g):
    return [jnp.where(g == 0, (0, 2, 6, 8)[e], 2 * e + 1) for e in range(4)]


def two_groups(body):
    def step(g, carry):
        body(group(g))
        return carry

    lax.fori_loop(0, 2, step, 0)


SIDES = (7, 1, 5, 3)


def greet():
    barrier = pltpu.get_barrier_semaphore()
    count = 0
    for d in (0, 1, 2, 3, 5, 6, 7, 8):
        there, target = neighbour(d)

        @pl.when(there)
        def _():
            pl.semaphore_signal(barrier, inc=1, device_id=target, device_id_type=MESH)

        count = count + there.astype(jnp.int32)
    return barrier, count


def halo_copy(src, dst, k, count, send_sem, recv_sem):
    return pltpu.make_async_remote_copy(
        src_ref=src.at[k, pl.ds(0, count)],
        dst_ref=dst.at[k, pl.ds(0, count)],
        send_sem=send_sem.at[k],
        recv_sem=recv_sem.at[k],
        device_id=neighbour(SIDES[k])[1],
        device_id_type=MESH,
    )


def fault_copy(src, dst, d, send_sem, recv_sem, back):
    return pltpu.make_async_remote_copy(
        src_ref=src.at[d],
        dst_ref=dst.at[back],
        send_sem=send_sem.at[d],
        recv_sem=recv_sem.at[back],
        device_id=neighbour(d)[1],
        device_id_type=MESH,
    )


def wait_halos(src, dst, counts, send_sem, recv_sem):
    for k in range(4):
        copy = halo_copy(src, dst, k, counts[k], send_sem, recv_sem)
        pl.when(neighbour(SIDES[k])[0])(copy.wait_send)
        pl.when(neighbour(8 - SIDES[k])[0])(copy.wait_recv)


def send_group(src, dst, ds, send_sem, recv_sem):
    for d in ds:
        pl.when(neighbour(d)[0])(fault_copy(src, dst, d, send_sem, recv_sem, 8 - d).start)


def wait_group(src, dst, ds, send_sem, recv_sem):
    for d in ds:
        copy = fault_copy(src, dst, d, send_sem, recv_sem, d)

        @pl.when(neighbour(d)[0])
        def _():
            copy.wait_send()
            copy.wait_recv()


def clear_missing(hrecv, rbuf):
    for k in range(4):

        @pl.when(jnp.logical_not(neighbour(8 - SIDES[k])[0]))
        def _():
            hrecv[k] = jnp.zeros_like(hrecv[k])

    def one(d, carry):
        @pl.when(jnp.logical_not(neighbour(d)[0]) | (d == 4))
        def _():
            rbuf[d] = jnp.zeros_like(rbuf[d])

        return carry

    lax.fori_loop(0, 9, one, 0)


def cell_rows(column, layer):
    return (column >> 4) * 8 + (column & 7), ((column >> 3) & 1) * 128 + layer


def hot(index, size):
    slots = index.shape[1]
    row = jnp.broadcast_to(index.astype(F32), (16, slots)).astype(BF16)
    iota = lax.broadcasted_iota(jnp.int32, (size, slots), 0).astype(F32).astype(BF16)
    return iota.reshape(size // 16, 16, slots) == row[None]


def hot_values(mask, value_row):
    slots = value_row.shape[1]
    hi, lo = split(jnp.broadcast_to(value_row, (16, slots)))
    zero = jnp.zeros((), BF16)
    return [jnp.where(mask, v[None], zero).reshape(128, slots) for v in (hi, lo)]


def hot_ones(mask):
    size = mask.shape[0] * 16
    return jnp.where(mask, jnp.ones((), BF16), jnp.zeros((), BF16)).reshape(size, mask.shape[2])


def lanes(parts):
    return jnp.concatenate(parts, axis=1)


def rows(parts):
    return jnp.concatenate(parts, axis=0)


def as_rows(x):
    return lanes([x[:, 0:8, :].reshape(128, 128), x[:, 8:16, :].reshape(128, 128)])


def dot_slots(weighted, put):
    return lax.dot_general(weighted, put, (((1,), (1,)), ((), ())), preferred_element_type=F32)


def gather(pieces, count, row_ref, lane_ref, d, store):
    for c in range(0, 8, 2):
        pick = lanes([hot_ones(hot(lane_ref[d, pl.ds(q, 1), :], 256)) for q in (c, c + 1)])
        lines = None
        for piece in pieces:
            line = jnp.dot(piece, pick, preferred_element_type=F32)
            lines = line if lines is None else lines + line
        for s in range(2):
            mask = lax.broadcasted_iota(jnp.int32, (128, 128), 0) == row_ref[d, pl.ds(c + s, 1), :]
            for f in range(count):
                part = lines[f * 128 : (f + 1) * 128, s * 128 : (s + 1) * 128]
                if len(pieces) == 1:
                    at = (count + f) * 128
                    part = part + lines[at : at + 128, s * 128 : (s + 1) * 128]
                store(f, c + s, jnp.sum(jnp.where(mask, part, 0.0), axis=0, keepdims=True))


def lower_side(values):
    return (-values[0], -values[1], values[2], values[3], values[4]) + tuple(-v for v in values[5:])


def exchange_kernel(
    p_hbm, sw_hbm, sg_hbm, z_hbm, t_hbm, fc_hbm, fl_hbm, ft_hbm,
    near_ref, far_ref, row_ref, lane_ref, ft_ref, blocks, acc, cond_ref, condlow_ref,
    x_ref, t_ref, fc_ref, fl_ref, sbuf, rbuf, hsend, hrecv, ghi, glo, lowj, in_sem, fs, fr, hs, hr,
):
    barrier, count = greet()
    loads = [pltpu.make_async_copy(fc_hbm, fc_ref, in_sem.at[0]), pltpu.make_async_copy(fl_hbm, fl_ref, in_sem.at[1])]
    for f, ref in enumerate((p_hbm, sw_hbm, sg_hbm, z_hbm)):
        loads.append(pltpu.make_async_copy(ref, x_ref.at[f], in_sem.at[2 + f]))
    loads.append(pltpu.make_async_copy(t_hbm, t_ref, in_sem.at[6]))
    loads.append(pltpu.make_async_copy(ft_hbm, ft_ref, in_sem.at[7]))
    for load in loads:
        load.start()
    clear_missing(hrecv, rbuf)
    sbuf[4] = jnp.zeros_like(sbuf[4])
    for load in loads[:2]:
        load.wait()
    row, lane = cell_rows(fc_ref[...], fl_ref[...])
    row_ref[...] = row
    lane_ref[...] = lane
    for load in loads[2:]:
        load.wait()
    for f in range(4):
        hsend[0, f] = x_ref[f, 15]
        hsend[1, f] = x_ref[f, 0]
        hsend[2, f] = x_ref[f, :, 15, :]
        hsend[3, f] = x_ref[f, :, 0, :]
    hsend[0, 4] = t_ref[0, 15]
    hsend[2, 4] = t_ref[1, :, 15, :]
    counts = (5, 4, 5, 4)
    for f in range(4):
        hi, lo = split(as_rows(x_ref[f]))
        ghi[pl.ds(f * 128, 128), :] = hi
        glo[pl.ds(f * 128, 128), :] = lo
    pl.semaphore_wait(barrier, count)
    for k in range(4):
        pl.when(neighbour(SIDES[k])[0])(halo_copy(hsend, hrecv, k, counts[k], hs, hr).start)

    def gather_group(ds):
        for d in ds:

            def store(f, q, value):
                sbuf[d, f, pl.ds(q, 1), :] = value

            gather([ghi[...], glo[...]], 4, row_ref, lane_ref, d, store)
        send_group(sbuf, rbuf, ds, fs, fr)

    two_groups(gather_group)
    wait_halos(hsend, hrecv, counts, hs, hr)

    def low_face(k, fields):
        a = [hrecv[k, f] for f in range(4)]
        values, _ = face_terms(
            hrecv[k, 4], cell_terms(*a[:3]), cell_terms(*fields[:3]), a[0], fields[0], a[3], fields[3]
        )
        condlow_ref[k // 2] = values[2] + values[3] + values[4]
        return lower_side(values)

    for v, value in enumerate(low_face(2, [x_ref[f, :, 0, :] for f in range(4)])):
        lowj[v] = value
    carry = low_face(0, [x_ref[f, 0] for f in range(4)])
    row_id = lax.broadcasted_iota(jnp.int32, (16, 128), 0)
    lane_id = lax.broadcasted_iota(jnp.int32, (16, 128), 1)
    keep_i = jnp.where(neighbour(SIDES[0])[0], 1.0, 0.0)
    keep_j = jnp.where(neighbour(SIDES[2])[0], 1.0, 0.0)

    def plane(i, carry):
        own = [x_ref[f, i] for f in range(4)]
        a = cell_terms(*own[:3])
        last = i == 15
        after = jnp.minimum(i + 1, 15)
        total = list(carry)
        out_carry = None
        for n in range(3):
            t = t_ref[n, i]
            if n == 0:
                nxt = [jnp.where(last, hrecv[1, f], x_ref[f, after]) for f in range(4)]
                t = t * jnp.where(last, keep_i, 1.0)
            elif n == 1:
                nxt = [
                    jnp.where(row_id == 15, hrecv[3, f, pl.ds(i, 1), :], pltpu.roll(own[f], 15, 0))
                    for f in range(4)
                ]
                t = jnp.where(row_id == 15, t * keep_j, t)
            else:
                nxt = [pltpu.roll(own[f], 127, 1) for f in range(4)]
                t = jnp.where(lane_id == 127, 0.0, t)
            b = cell_terms(*nxt[:3])
            values, (ww, wo, wg) = face_terms(t, a, b, own[0], nxt[0], own[3], nxt[3])
            mw, mo, mgd = values[2:5]
            cond_ref[n, i] = mw + mo + mgd
            upper = block_rows(b, ww, wo, wg, -mw, -mo, -mgd)
            lower = block_rows(a, -ww, -wo, -wg, -mw, -mo, -mgd)
            for e in range(9):
                blocks[n, 0, e, i] = upper[e].astype(BF16)
                blocks[n, 1, e, i] = lower[e].astype(BF16)
            total = [x + y for x, y in zip(total, values)]
            below = lower_side(values)
            if n == 0:
                out_carry = below
            elif n == 1:
                for v in range(8):
                    shifted = jnp.where(row_id == 0, lowj[v, pl.ds(i, 1), :], pltpu.roll(below[v], 1, 0))
                    total[v] = total[v] + shifted
            else:
                total = [x + pltpu.roll(y, 1, 1) for x, y in zip(total, below)]
        for v in range(8):
            at = pl.multiple_of(v * 128 + i * 8, 8)
            acc[pl.ds(at, 8), 0:128] = total[v][0:8]
            acc[pl.ds(at, 8), 128:256] = total[v][8:16]
        return tuple(out_carry)

    lax.fori_loop(0, 16, plane, tuple(carry))
    two_groups(lambda ds: wait_group(sbuf, rbuf, ds, fs, fr))
    near_ref[...] = sbuf[...]
    far_ref[...] = rbuf[...]


def terms_kernel(
    near_ref, far_ref, row_ref, lane_ref, ft_ref, blocks, face_acc,
    p_hbm, sw_hbm, sg_hbm, pv_hbm, om_hbm, pc_hbm, wi_hbm, wp_hbm,
    res_ref, diag_ref, face_hbm, fault_ref, first_ref, rhs_ref, pd_ref, fcond_ref,
    x_ref, om_ref, w_ref, pc_ref, acc, wacc, chan, fault_rows, in_sem, out_sem,
):
    out_copy = pltpu.make_async_copy(blocks, face_hbm, out_sem)
    loads = [pltpu.make_async_copy(pc_hbm, pc_ref, in_sem.at[0]), pltpu.make_async_copy(om_hbm, om_ref, in_sem.at[1])]
    for f, ref in enumerate((p_hbm, sw_hbm, sg_hbm, pv_hbm)):
        loads.append(pltpu.make_async_copy(ref, x_ref.at[f], in_sem.at[2 + f]))
    for f, ref in enumerate((wi_hbm, wp_hbm)):
        loads.append(pltpu.make_async_copy(ref, w_ref.at[f], in_sem.at[6 + f]))
    for load in loads:
        load.start()
    out_copy.start()

    near = [near_ref[:, f].reshape(72, 128) for f in range(4)]
    far = [far_ref[:, f].reshape(72, 128) for f in range(4)]
    a, b = cell_terms(*near[:3]), cell_terms(*far[:3])
    values, (ww, wo, wg) = face_terms(
        ft_ref[...].reshape(72, 128), a, b, near[0], far[0], near[3], far[3]
    )
    mw, mo, mgd = values[2:5]
    fcond_ref[...] = (mw + mo + mgd).reshape(9, 8, 128)
    for v in range(8):
        chan[v] = values[v].reshape(9, 8, 128)
    for e, value in enumerate(block_rows(b, ww, wo, wg, -mw, -mo, -mgd)):
        fault_rows[e] = value
    acc[...] = face_acc[...]

    def scatter_group(ds):
        for d in ds:
            for c in range(0, 8, 2):
                pair = (c, c + 1)
                put = lanes([hot_ones(hot(lane_ref[d, pl.ds(q, 1), :], 256)) for q in pair])
                masks = [hot(row_ref[d, pl.ds(q, 1), :], 128) for q in pair]
                his, los = [], []
                for v in range(8):
                    both = [hot_values(m, chan[v, d, pl.ds(q, 1), :]) for m, q in zip(masks, pair)]
                    his.append(lanes([x[0] for x in both]))
                    los.append(lanes([x[1] for x in both]))
                acc[...] += dot_slots(lanes([rows(his), rows(los)]), lanes([put, put]))

    two_groups(scatter_group)

    def fault_out(e, carry):
        for di in range(3):
            for q in range(8):
                line = fault_rows[e, pl.ds(di * 24 + q, 3, 8), :]
                fault_ref[e, 0, di, :, pl.ds(q * 128, 128)] = line.astype(BF16)
        return carry

    lax.fori_loop(0, 9, fault_out, 0)
    for load in loads:
        load.wait()
    cell = pc_ref[...]
    row, lane = cell_rows(cell >> 7, cell & 127)
    mask = hot(row, 128)
    hi_w, lo_w = hot_values(mask, w_ref[0])
    hi_q, lo_q = hot_values(mask, w_ref[0] * w_ref[1])
    put = hot_ones(hot(lane, 256))
    wacc[...] = dot_slots(lanes([rows([hi_w, hi_q]), rows([lo_w, lo_q])]), lanes([put, put]))

    def rows_of(ref, start):
        at = pl.multiple_of(start, 8)
        return rows([ref[pl.ds(at, 8), 0:128], ref[pl.ds(at, 8), 128:256]])

    def finish(i, carry):
        p, sw, sg = x_ref[0, i], x_ref[1, i], x_ref[2, i]
        c = cell_terms(p, sw, sg)
        hp, hz, mw, mo, mgd, rw, ro, rg = [rows_of(acc, v * 128 + i * 8) for v in range(8)]
        well = rows_of(wacc, i * 8)
        drive = rows_of(wacc, 128 + i * 8) - p * well
        oil = 1.0 - sw - sg
        pv = x_ref[3, i]
        rock = 2.0 * (pv * (1.0 + 0.02 * p))
        rock_p = 0.04 * pv
        bw, bo, bg, rs = 1.0 + 0.05 * p, 1.0 + 0.1 * p, 1.0 + 0.4 * p, 0.5 + 0.2 * p
        ob = oil * bo
        gas = sg * bg + rs * ob
        r0 = rock * sw * bw - 2.0 * om_ref[0, i] + rw - drive * c["mw"]
        r1 = rock * ob - 2.0 * om_ref[1, i] + ro - drive * c["mo"]
        r2 = rock * gas - 2.0 * om_ref[2, i] + rg - drive * (c["mg"] + c["md"])
        res_ref[0, i], res_ref[1, i], res_ref[2, i] = r0, r1, r2
        a0 = rock_p * sw * bw + rock * sw * 0.05
        a3 = rock_p * ob + rock * oil * 0.1
        a6 = rock_p * gas + rock * (0.4 * sg + 0.2 * ob + 0.1 * rs * oil)
        total = c["mw"] + c["mo"] + c["mg"] + c["md"]
        pd = a0 + a3 + a6 + mw + mo + mgd + well * total
        dw = hp - 0.1 * hz - drive
        do = hp - 0.08 * hz - drive
        dg = hp - 0.02 * hz - drive
        solved = c["md_o"] * do
        pair = -(rock * bo) - c["mo_o"] * do
        gas_water = -(rock * rs * bo) - solved
        out = (
            a0 + c["mw_p"] * dw + mw + well * c["mw"],
            rock * bw + c["mw_s"] * dw,
            jnp.zeros_like(p),
            a3 + c["mo_p"] * do + mo + well * c["mo"],
            pair,
            pair,
            a6 + c["mg_p"] * dg + c["md_p"] * do + mgd + well * (c["mg"] + c["md"]),
            gas_water,
            rock * bg + c["mg_s"] * dg + gas_water,
        )
        for e in range(9):
            diag_ref[e, i] = out[e].astype(BF16)
        rhs = -(r0 + r1 + r2)
        rhs_ref[i] = rhs
        pd_ref[i] = pd
        first_ref[i] = rhs / pd
        return carry

    lax.fori_loop(0, 16, finish, 0)
    out_copy.wait()


def update_kernel(
    first_ref, rhs_ref, pd_ref, cond_ref, condlow_ref, fcond_ref, row_ref, lane_ref,
    out_ref,
    sbuf, rbuf, hsend, hrecv, ghl, acc, fs, fr, hs, hr,
):
    barrier, count = greet()
    hsend[0, 0] = first_ref[15]
    hsend[1, 0] = first_ref[0]
    hsend[2, 0] = first_ref[:, 15, :]
    hsend[3, 0] = first_ref[:, 0, :]
    counts = (1, 1, 1, 1)
    clear_missing(hrecv, rbuf)
    hi, lo = split(as_rows(first_ref[...]))
    ghl[0:128, :] = hi
    ghl[128:256, :] = lo
    pl.semaphore_wait(barrier, count)
    for k in range(4):
        pl.when(neighbour(SIDES[k])[0])(halo_copy(hsend, hrecv, k, 1, hs, hr).start)

    def gather_group(ds):
        for d in ds:

            def store(f, q, value):
                sbuf[d, pl.ds(q, 1), :] = value

            gather([ghl[...]], 1, row_ref, lane_ref, d, store)
        send_group(sbuf, rbuf, ds, fs, fr)

    two_groups(gather_group)
    wait_halos(hsend, hrecv, counts, hs, hr)
    row_id = lax.broadcasted_iota(jnp.int32, (16, 128), 0)

    def faces(i, carry):
        own = first_ref[i]
        before, after = jnp.maximum(i - 1, 0), jnp.minimum(i + 1, 15)
        up = jnp.where(i == 15, hrecv[1, 0], first_ref[after])
        down = jnp.where(i == 0, hrecv[0, 0], first_ref[before])
        total = cond_ref[0, i] * up
        total += jnp.where(i == 0, condlow_ref[0], cond_ref[0, before]) * down
        cj = cond_ref[1, i]
        up = jnp.where(row_id == 15, hrecv[3, 0, pl.ds(i, 1), :], pltpu.roll(own, 15, 0))
        down = jnp.where(row_id == 0, hrecv[2, 0, pl.ds(i, 1), :], pltpu.roll(own, 1, 0))
        cj_low = jnp.where(row_id == 0, condlow_ref[1, pl.ds(i, 1), :], pltpu.roll(cj, 1, 0))
        total += cj * up + cj_low * down
        ck = cond_ref[2, i]
        total += ck * pltpu.roll(own, 127, 1) + pltpu.roll(ck * own, 1, 1)
        at = pl.multiple_of(i * 8, 8)
        acc[pl.ds(at, 8), 0:128] = total[0:8]
        acc[pl.ds(at, 8), 128:256] = total[8:16]
        return carry

    lax.fori_loop(0, 16, faces, 0)
    acc[128:256, :] = jnp.zeros((128, 256), F32)

    def scatter_group(ds):
        wait_group(sbuf, rbuf, ds, fs, fr)
        for d in ds:
            values = fcond_ref[d] * rbuf[d]
            for c in range(0, 8, 2):
                pair = (c, c + 1)
                put = lanes([hot_ones(hot(lane_ref[d, pl.ds(q, 1), :], 256)) for q in pair])
                both = [
                    hot_values(hot(row_ref[d, pl.ds(q, 1), :], 128), values[q : q + 1]) for q in pair
                ]
                weighted = rows([lanes([x[0] for x in both]), lanes([x[1] for x in both])])
                acc[...] += dot_slots(weighted, put)

    two_groups(scatter_group)

    def finish(i, carry):
        at = pl.multiple_of(i * 8, 8)
        total = acc[pl.ds(at, 8), :] + acc[pl.ds(at + 128, 8), :]
        total = rows([total[:, 0:128], total[:, 128:256]])
        out_ref[i] = (rhs_ref[i] + total) / pd_ref[i]
        return carry

    lax.fori_loop(0, 16, finish, 0)


def in_vmem(count):
    return [pl.BlockSpec(memory_space=pltpu.VMEM)] * count


def in_hbm(count):
    return [pl.BlockSpec(memory_space=pltpu.HBM)] * count


def per_device(p, sw, sg, z, pv, om, t, fc, fl, ft, pc, wi, wp):
    def dense(x):
        return jnp.transpose(x, (1, 2, 0, 3)).reshape(9, 8, 128)

    def f32(*shape):
        return jax.ShapeDtypeStruct(shape, F32)

    slots = fc.shape[3]
    cells = p.shape
    fc, fl, ft = dense(fc), dense(fl), dense(ft)
    p, sw, sg, z, pv, om, t, fc, fl, ft, pc, wi, wp = [
        pltpu.with_memory_space_constraint(x, pltpu.HBM)
        for x in (p, sw, sg, z, pv, om, t, fc, fl, ft, pc, wi, wp)
    ]
    dma = pltpu.SemaphoreType.DMA
    index = jax.ShapeDtypeStruct((9, 8, 128), jnp.int32)
    near, far, row, lane, ft_dense, blocks, acc, cond, condlow = pl.pallas_call(
        exchange_kernel,
        out_shape=[
            f32(9, 4, 8, 128),
            f32(9, 4, 8, 128),
            index,
            index,
            f32(9, 8, 128),
            jax.ShapeDtypeStruct((3, 2, 9) + cells, BF16),
            f32(1024, 256),
            f32(3, *cells),
            f32(2, 16, 128),
        ],
        in_specs=in_hbm(8),
        out_specs=in_vmem(9),
        scratch_shapes=[
            pltpu.VMEM((4,) + cells, F32),
            pltpu.VMEM((3,) + cells, F32),
            pltpu.VMEM((9, 8, 128), jnp.int32),
            pltpu.VMEM((9, 8, 128), jnp.int32),
            pltpu.VMEM((9, 4, 8, 128), F32),
            pltpu.VMEM((9, 4, 8, 128), F32),
            pltpu.VMEM((4, 5, 16, 128), F32),
            pltpu.VMEM((4, 5, 16, 128), F32),
            pltpu.VMEM((512, 256), BF16),
            pltpu.VMEM((512, 256), BF16),
            pltpu.VMEM((8, 16, 128), F32),
            dma((8,)),
            dma((9,)),
            dma((9,)),
            dma((4,)),
            dma((4,)),
        ],
        compiler_params=pltpu.CompilerParams(
            collective_id=0, has_side_effects=True, vmem_limit_bytes=VMEM_BYTES
        ),
        name="exchange",
    )(p, sw, sg, z, t, fc, fl, ft)
    res, diag, face, fault, first, rhs, pd, fcond = pl.pallas_call(
        terms_kernel,
        out_shape=[
            f32(3, *cells),
            jax.ShapeDtypeStruct((9,) + cells, BF16),
            jax.ShapeDtypeStruct((3, 2, 9) + cells, BF16),
            jax.ShapeDtypeStruct((9, 1, 3, 3, slots), BF16),
            f32(*cells),
            f32(*cells),
            f32(*cells),
            f32(9, 8, 128),
        ],
        in_specs=in_vmem(7) + in_hbm(8),
        out_specs=in_vmem(2) + in_hbm(1) + in_vmem(5),
        scratch_shapes=[
            pltpu.VMEM((4,) + cells, F32),
            pltpu.VMEM((3,) + cells, F32),
            pltpu.VMEM((2, 1, 128), F32),
            pltpu.VMEM((1, 128), jnp.int32),
            pltpu.VMEM((1024, 256), F32),
            pltpu.VMEM((256, 256), F32),
            pltpu.VMEM((8, 9, 8, 128), F32),
            pltpu.VMEM((9, 72, 128), F32),
            dma((8,)),
            dma,
        ],
        compiler_params=pltpu.CompilerParams(vmem_limit_bytes=VMEM_BYTES),
        name="terms",
    )(near, far, row, lane, ft_dense, blocks, acc, p, sw, sg, pv, om, pc, wi, wp)
    update = pl.pallas_call(
        update_kernel,
        out_shape=f32(*cells),
        in_specs=in_vmem(8),
        out_specs=in_vmem(1)[0],
        scratch_shapes=[
            pltpu.VMEM((9, 8, 128), F32),
            pltpu.VMEM((9, 8, 128), F32),
            pltpu.VMEM((4, 1, 16, 128), F32),
            pltpu.VMEM((4, 1, 16, 128), F32),
            pltpu.VMEM((256, 256), BF16),
            pltpu.VMEM((256, 256), F32),
            dma((9,)),
            dma((9,)),
            dma((4,)),
            dma((4,)),
        ],
        compiler_params=pltpu.CompilerParams(
            collective_id=1, has_side_effects=True, vmem_limit_bytes=VMEM_BYTES
        ),
        name="update",
    )(first, rhs, pd, cond, condlow, fcond, row, lane)
    return res, diag, face, fault, update


def solution(mesh):
    cells = P("col", "row", None)
    stacked = P(None, "col", "row", None)
    owned = P(("col", "row"), None, None, None)
    wells = P(("col", "row"), None)
    return jax.shard_map(
        per_device,
        mesh=mesh,
        in_specs=(cells,) * 5 + (stacked,) * 2 + (owned,) * 3 + (wells,) * 3,
        out_specs=(
            stacked,
            stacked,
            P(None, None, None, "col", "row", None),
            P(None, ("col", "row"), None, None, None),
            cells,
        ),
        check_vma=False,
    )
```

```python
import jax
import jax.numpy as jnp
from jax import lax
from jax.experimental import pallas as pl
from jax.experimental.pallas import tpu as pltpu
from jax.sharding import PartitionSpec as P

F32 = jnp.float32
BF16 = jnp.bfloat16
MESH = pl.DeviceIdType.MESH
VMEM_BYTES = 40 * 1024 * 1024


def split(x):
    hi = x.astype(BF16)
    return hi, (x - hi.astype(F32)).astype(BF16)


def cell_terms(p, sw, sg):
    oil = 1.0 - sw - sg
    bw = 1.0 + 0.05 * p
    bo = 1.0 + 0.1 * p
    bg = 1.0 + 0.4 * p
    rs = 0.5 + 0.2 * p
    w2 = sw * (sw * (1.0 / 0.3))
    o2 = oil * (oil * (1.0 / 0.8))
    g2 = sg * (sg * (1.0 / 0.05))
    mo = bo * o2
    mo_p = 0.1 * o2
    mo_o = bo * (oil * (2.0 / 0.8))
    return dict(
        mw=bw * w2,
        mo=mo,
        mg=bg * g2,
        md=rs * mo,
        mw_p=0.05 * w2,
        mw_s=bw * (sw * (2.0 / 0.3)),
        mo_p=mo_p,
        mo_o=mo_o,
        mg_p=0.4 * g2,
        mg_s=bg * (sg * (2.0 / 0.05)),
        md_p=0.2 * mo + rs * mo_p,
        md_o=rs * mo_o,
    )


def face_terms(t, a, b, pa, pb, za, zb):
    half = 0.5 * t
    hp = half * (pa - pb)
    hz = half * (za - zb)
    ww = hp - 0.1 * hz
    wo = hp - 0.08 * hz
    wg = hp - 0.02 * hz
    sum_w = a["mw"] + b["mw"]
    sum_o = a["mo"] + b["mo"]
    sum_g = a["mg"] + b["mg"]
    sum_d = a["md"] + b["md"]
    mw = half * sum_w
    mo = half * sum_o
    mgd = half * (sum_g + sum_d)
    flux = (sum_w * ww, sum_o * wo, sum_g * wg + sum_d * wo)
    return (hp, hz, mw, mo, mgd) + flux, (ww, wo, wg)


def block_rows(c, ww, wo, wg, mw, mo, mgd):
    oil = c["mo_o"] * wo
    solved = c["md_o"] * wo
    zero = jnp.zeros_like(ww)
    return (
        c["mw_p"] * ww + mw,
        c["mw_s"] * ww,
        zero,
        c["mo_p"] * wo + mo,
        -oil,
        -oil,
        c["mg_p"] * wg + c["md_p"] * wo + mgd,
        -solved,
        c["mg_s"] * wg - solved,
    )


def neighbour(d):
    a, b = lax.axis_index("col"), lax.axis_index("row")
    ta, tb = a + d // 3 - 1, b + d % 3 - 1
    na, nb = lax.axis_size("col"), lax.axis_size("row")
    there = (ta >= 0) & (ta < na) & (tb >= 0) & (tb < nb)
    return there, (ta, tb)


def direction(g, h, u):
    return jnp.where(g == 0, 2 * u + 6 * h, 4 * h + 2 * u + 1)


def group(g):
    return [direction(g, h, u) for h in range(2) for u in range(2)]


def two_groups(body):
    def step(g, carry):
        body(group(g))
        return carry

    lax.fori_loop(0, 2, step, 0)


SIDES = (7, 1, 5, 3)


def greet():
    barrier = pltpu.get_barrier_semaphore()
    count = 0
    for d in (0, 1, 2, 3, 5, 6, 7, 8):
        there, target = neighbour(d)

        @pl.when(there)
        def _():
            pl.semaphore_signal(barrier, inc=1, device_id=target, device_id_type=MESH)

        count = count + there.astype(jnp.int32)
    return barrier, count


def halo_copy(src, dst, k, count, send_sem, recv_sem):
    return pltpu.make_async_remote_copy(
        src_ref=src.at[k, pl.ds(0, count)],
        dst_ref=dst.at[k, pl.ds(0, count)],
        send_sem=send_sem.at[k],
        recv_sem=recv_sem.at[k],
        device_id=neighbour(SIDES[k])[1],
        device_id_type=MESH,
    )


def fault_copy(src, dst, d, send_sem, recv_sem, back):
    return pltpu.make_async_remote_copy(
        src_ref=src.at[d],
        dst_ref=dst.at[back],
        send_sem=send_sem.at[d],
        recv_sem=recv_sem.at[back],
        device_id=neighbour(d)[1],
        device_id_type=MESH,
    )


def wait_halos(src, dst, counts, send_sem, recv_sem):
    for k in range(4):
        copy = halo_copy(src, dst, k, counts[k], send_sem, recv_sem)
        pl.when(neighbour(SIDES[k])[0])(copy.wait_send)
        pl.when(neighbour(8 - SIDES[k])[0])(copy.wait_recv)


def send_group(src, dst, ds, send_sem, recv_sem):
    for d in ds:
        pl.when(neighbour(d)[0])(fault_copy(src, dst, d, send_sem, recv_sem, 8 - d).start)


def wait_group(src, dst, ds, send_sem, recv_sem):
    for d in ds:
        copy = fault_copy(src, dst, d, send_sem, recv_sem, d)

        @pl.when(neighbour(d)[0])
        def _():
            copy.wait_send()
            copy.wait_recv()


def clear_missing(hrecv, rbuf):
    for k in range(4):

        @pl.when(jnp.logical_not(neighbour(8 - SIDES[k])[0]))
        def _():
            hrecv[k] = jnp.zeros_like(hrecv[k])

    def one(d, carry):
        @pl.when(jnp.logical_not(neighbour(d)[0]) | (d == 4))
        def _():
            rbuf[d] = jnp.zeros_like(rbuf[d])

        return carry

    lax.fori_loop(0, 9, one, 0)


def cell_rows(column, layer):
    return (column >> 4) * 8 + (column & 7), ((column >> 3) & 1) * 128 + layer


def hot(index, size):
    slots = index.shape[1]
    row = jnp.broadcast_to(index.astype(F32), (16, slots)).astype(BF16)
    iota = lax.broadcasted_iota(jnp.int32, (size, slots), 0).astype(F32).astype(BF16)
    return iota.reshape(size // 16, 16, slots) == row[None]


def hot_values(mask, value_row):
    slots = value_row.shape[1]
    hi, lo = split(jnp.broadcast_to(value_row, (16, slots)))
    zero = jnp.zeros((), BF16)
    return [jnp.where(mask, v[None], zero).reshape(128, slots) for v in (hi, lo)]


def hot_ones(mask):
    size = mask.shape[0] * 16
    return jnp.where(mask, jnp.ones((), BF16), jnp.zeros((), BF16)).reshape(size, mask.shape[2])


def lanes(parts):
    return jnp.concatenate(parts, axis=1)


def rows(parts):
    return jnp.concatenate(parts, axis=0)


def as_rows(x):
    return lanes([x[:, 0:8, :].reshape(128, 128), x[:, 8:16, :].reshape(128, 128)])


def dot_slots(weighted, put):
    return lax.dot_general(weighted, put, (((1,), (1,)), ((), ())), preferred_element_type=F32)


def gather(pieces, count, row_ref, lane_ref, d, store):
    for c in range(0, 8, 2):
        pick = lanes([hot_ones(hot(lane_ref[d, pl.ds(q, 1), :], 256)) for q in (c, c + 1)])
        lines = None
        for piece in pieces:
            line = jnp.dot(piece, pick, preferred_element_type=F32)
            lines = line if lines is None else lines + line
        for s in range(2):
            mask = lax.broadcasted_iota(jnp.int32, (128, 128), 0) == row_ref[d, pl.ds(c + s, 1), :]
            for f in range(count):
                part = lines[f * 128 : (f + 1) * 128, s * 128 : (s + 1) * 128]
                if len(pieces) == 1:
                    at = (count + f) * 128
                    part = part + lines[at : at + 128, s * 128 : (s + 1) * 128]
                store(f, c + s, jnp.sum(jnp.where(mask, part, 0.0), axis=0, keepdims=True))


def lower_side(values):
    return (-values[0], -values[1], values[2], values[3], values[4]) + tuple(-v for v in values[5:])


def plane_loop(body):
    def step(i, carry):
        body(2 * i)
        body(2 * i + 1)
        return carry

    lax.fori_loop(0, 8, step, 0)


def rows_of(ref, start):
    at = pl.multiple_of(start, 8)
    return rows([ref[pl.ds(at, 8), 0:128], ref[pl.ds(at, 8), 128:256]])


def scatter_first(ds, row_ref, lane_ref, fcond_ref, far_ref, acc2):
    for d in ds:
        values = fcond_ref[d] * far_ref[d]
        for c in range(0, 8, 2):
            pair = (c, c + 1)
            put = lanes([hot_ones(hot(lane_ref[d, pl.ds(q, 1), :], 256)) for q in pair])
            both = [hot_values(hot(row_ref[d, pl.ds(q, 1), :], 128), values[q : q + 1]) for q in pair]
            weighted = rows([lanes([x[0] for x in both]), lanes([x[1] for x in both])])
            acc2[...] += dot_slots(weighted, put)


def system_kernel(
    p_hbm, sw_hbm, sg_hbm, z_hbm, pv_hbm, om_hbm, t_hbm, fc_hbm, fl_hbm, ft_hbm, pc_hbm, wi_hbm, wp_hbm,
    blocks, res_ref, diag_ref, fault_ref, rhs_ref, pd_ref, acc2, far2, fcond_ref, row_ref, lane_ref,
    x_ref, t_ref, om_ref, fc_ref, fl_ref, ft_ref, pc_ref, w_ref, sbuf, rbuf, hsend, hrecv, ghi, glo, lowj,
    carry_ref, acc, fa, wacc, chan, fault_rows, cond_ref, condlow_ref, first_ref, sbuf2, rbuf2, hsend2, hrecv2, ghl,
    in_sem, fs, fr, hs, hr, fs2, fr2, hs2, hr2,
):
    barrier, count = greet()
    pairs = [(fc_hbm, fc_ref), (fl_hbm, fl_ref)]
    pairs += [(ref, x_ref.at[f]) for f, ref in enumerate((p_hbm, sw_hbm, sg_hbm, z_hbm))]
    pairs += [(t_hbm, t_ref), (ft_hbm, ft_ref), (pc_hbm, pc_ref), (wi_hbm, w_ref.at[0]), (wp_hbm, w_ref.at[1])]
    pairs += [(pv_hbm, x_ref.at[4]), (om_hbm, om_ref)]
    loads = [pltpu.make_async_copy(a, b, in_sem.at[n]) for n, (a, b) in enumerate(pairs)]
    for load in loads:
        load.start()
    clear_missing(hrecv, rbuf)
    clear_missing(hrecv2, rbuf2)
    fault_rows[:, 32:40, :] = jnp.zeros((9, 8, 128), F32)
    fcond_ref[4] = jnp.zeros((8, 128), F32)
    acc[...] = jnp.zeros_like(acc)
    for load in loads[:2]:
        load.wait()
    row, lane = cell_rows(fc_ref[...], fl_ref[...])
    row_ref[...] = row
    lane_ref[...] = lane
    for load in loads[2:7]:
        load.wait()
    for f in range(4):
        hsend[0, f] = x_ref[f, 15]
        hsend[1, f] = x_ref[f, 0]
        hsend[2, f] = x_ref[f, :, 15, :]
        hsend[3, f] = x_ref[f, :, 0, :]
    hsend[0, 4] = t_ref[0, 15]
    hsend[2, 4] = t_ref[1, :, 15, :]
    counts = (5, 4, 5, 4)
    for f in range(4):
        hi, lo = split(as_rows(x_ref[f]))
        ghi[pl.ds(f * 128, 128), :] = hi
        glo[pl.ds(f * 128, 128), :] = lo
    pl.semaphore_wait(barrier, count)
    for k in range(4):
        pl.when(neighbour(SIDES[k])[0])(halo_copy(hsend, hrecv, k, counts[k], hs, hr).start)

    def gather_group(ds):
        for d in ds:

            def store(f, q, value):
                sbuf[d, f, pl.ds(q, 1), :] = value

            gather([ghi[...], glo[...]], 4, row_ref, lane_ref, d, store)
        send_group(sbuf, rbuf, ds, fs, fr)

    two_groups(gather_group)
    for load in loads[7:]:
        load.wait()
    wait_halos(hsend, hrecv, counts, hs, hr)

    def low_face(k, fields):
        a = [hrecv[k, f] for f in range(4)]
        values, _ = face_terms(
            hrecv[k, 4], cell_terms(*a[:3]), cell_terms(*fields[:3]), a[0], fields[0], a[3], fields[3]
        )
        condlow_ref[k // 2] = values[2] + values[3] + values[4]
        return lower_side(values)

    for v, value in enumerate(low_face(2, [x_ref[f, :, 0, :] for f in range(4)])):
        lowj[v] = value
    for v, value in enumerate(low_face(0, [x_ref[f, 0] for f in range(4)])):
        carry_ref[v] = value
    row_id = lax.broadcasted_iota(jnp.int32, (16, 128), 0)
    lane_id = lax.broadcasted_iota(jnp.int32, (16, 128), 1)
    keep_i = jnp.where(neighbour(SIDES[0])[0], 1.0, 0.0)
    keep_j = jnp.where(neighbour(SIDES[2])[0], 1.0, 0.0)

    def plane(i, carry):
        own = [x_ref[f, i] for f in range(4)]
        a = cell_terms(*own[:3])
        last = i == 15
        after = jnp.minimum(i + 1, 15)
        total = list(carry)
        out_carry = None
        for n in range(3):
            t = t_ref[n, i]
            if n == 0:
                nxt = [jnp.where(last, hrecv[1, f], x_ref[f, after]) for f in range(4)]
                t = t * jnp.where(last, keep_i, 1.0)
            elif n == 1:
                nxt = [
                    jnp.where(row_id == 15, hrecv[3, f, pl.ds(i, 1), :], pltpu.roll(own[f], 15, 0))
                    for f in range(4)
                ]
                t = jnp.where(row_id == 15, t * keep_j, t)
            else:
                nxt = [pltpu.roll(own[f], 127, 1) for f in range(4)]
                t = jnp.where(lane_id == 127, 0.0, t)
            b = cell_terms(*nxt[:3])
            values, (ww, wo, wg) = face_terms(t, a, b, own[0], nxt[0], own[3], nxt[3])
            mw, mo, mgd = values[2:5]
            cond_ref[n, i] = mw + mo + mgd
            upper = block_rows(b, ww, wo, wg, -mw, -mo, -mgd)
            lower = block_rows(a, -ww, -wo, -wg, -mw, -mo, -mgd)
            for e in range(9):
                blocks[n, 0, e, i] = upper[e].astype(BF16)
                blocks[n, 1, e, i] = lower[e].astype(BF16)
            total = [x + y for x, y in zip(total, values)]
            below = lower_side(values)
            if n == 0:
                out_carry = below
            elif n == 1:
                for v in range(8):
                    shifted = jnp.where(row_id == 0, lowj[v, pl.ds(i, 1), :], pltpu.roll(below[v], 1, 0))
                    total[v] = total[v] + shifted
            else:
                total = [x + pltpu.roll(y, 1, 1) for x, y in zip(total, below)]
        for v in range(8):
            fa[v, i] = total[v]
        return out_carry

    def fault_terms(d):
        near = [sbuf[d, f] for f in range(4)]
        far = [rbuf[d, f] for f in range(4)]
        a, b = cell_terms(*near[:3]), cell_terms(*far[:3])
        values, (ww, wo, wg) = face_terms(ft_ref[d], a, b, near[0], far[0], near[3], far[3])
        mw, mo, mgd = values[2:5]
        fcond_ref[d] = mw + mo + mgd
        for v in range(8):
            chan[v, d] = values[v]
        for e, value in enumerate(block_rows(b, ww, wo, wg, -mw, -mo, -mgd)):
            fault_rows[e, pl.ds(pl.multiple_of(d * 8, 8), 8), :] = value

    def scatter(d, c):
        pair = (c, c + 1)
        put = lanes([hot_ones(hot(lane_ref[d, pl.ds(q, 1), :], 256)) for q in pair])
        masks = [hot(row_ref[d, pl.ds(q, 1), :], 128) for q in pair]
        his, los = [], []
        for v in range(8):
            both = [hot_values(m, chan[v, d, pl.ds(q, 1), :]) for m, q in zip(masks, pair)]
            his.append(lanes([x[0] for x in both]))
            los.append(lanes([x[1] for x in both]))
        acc[...] += dot_slots(lanes([rows(his), rows(los)]), lanes([put, put]))

    def main_group(g, carry):
        wait_group(sbuf, rbuf, group(g), fs, fr)
        for d in group(g):
            fault_terms(d)

        def half(h, carry):
            below = [carry_ref[v] for v in range(8)]
            for u in range(2):
                for m in range(2):
                    for c in (4 * m, 4 * m + 2):
                        scatter(direction(g, h, u), c)
                    below = plane(g * 8 + h * 4 + u * 2 + m, below)
            for v in range(8):
                carry_ref[v] = below[v]
            return carry

        lax.fori_loop(0, 2, half, 0)
        return carry

    lax.fori_loop(0, 2, main_group, 0)

    cell = pc_ref[...]
    row, lane = cell_rows(cell >> 7, cell & 127)
    mask = hot(row, 128)
    hi_w, lo_w = hot_values(mask, w_ref[0])
    hi_q, lo_q = hot_values(mask, w_ref[0] * w_ref[1])
    put = hot_ones(hot(lane, 256))
    wacc[...] = dot_slots(lanes([rows([hi_w, hi_q]), rows([lo_w, lo_q])]), lanes([put, put]))

    def sums(i):
        return [fa[v, i] + rows_of(acc, v * 128 + i * 8) for v in range(8)]

    def accumulation(i):
        p, sw, sg = x_ref[0, i], x_ref[1, i], x_ref[2, i]
        well = rows_of(wacc, i * 8)
        drive = rows_of(wacc, 128 + i * 8) - p * well
        oil = 1.0 - sw - sg
        pv = x_ref[4, i]
        rock = 2.0 * (pv * (1.0 + 0.02 * p))
        rock_p = 0.04 * pv
        bw, bo, bg, rs = 1.0 + 0.05 * p, 1.0 + 0.1 * p, 1.0 + 0.4 * p, 0.5 + 0.2 * p
        ob = oil * bo
        gas = sg * bg + rs * ob
        a0 = rock_p * sw * bw + rock * sw * 0.05
        a3 = rock_p * ob + rock * oil * 0.1
        a6 = rock_p * gas + rock * (0.4 * sg + 0.2 * ob + 0.1 * rs * oil)
        return cell_terms(p, sw, sg), well, drive, rock, (rock * sw * bw, rock * ob, rock * gas), (a0, a3, a6), (bw, bo, bg, rs)

    def residuals(i):
        _, _, mw, mo, mgd, rw, ro, rg = sums(i)
        c, well, drive, rock, held, slope, _ = accumulation(i)
        r0 = held[0] - 2.0 * om_ref[0, i] + rw - drive * c["mw"]
        r1 = held[1] - 2.0 * om_ref[1, i] + ro - drive * c["mo"]
        r2 = held[2] - 2.0 * om_ref[2, i] + rg - drive * (c["mg"] + c["md"])
        res_ref[0, i], res_ref[1, i], res_ref[2, i] = r0, r1, r2
        total = c["mw"] + c["mo"] + c["mg"] + c["md"]
        pd = slope[0] + slope[1] + slope[2] + mw + mo + mgd + well * total
        rhs = -(r0 + r1 + r2)
        rhs_ref[i] = rhs
        pd_ref[i] = pd
        first_ref[i] = rhs / pd

    def diagonals(i):
        hp, hz, mw, mo, mgd, _, _, _ = sums(i)
        c, well, drive, rock, held, slope, (bw, bo, bg, rs) = accumulation(i)
        dw = hp - 0.1 * hz - drive
        do = hp - 0.08 * hz - drive
        dg = hp - 0.02 * hz - drive
        pair = -(rock * bo) - c["mo_o"] * do
        gas_water = -(rock * rs * bo) - c["md_o"] * do
        out = (
            slope[0] + c["mw_p"] * dw + mw + well * c["mw"],
            rock * bw + c["mw_s"] * dw,
            jnp.zeros_like(dw),
            slope[1] + c["mo_p"] * do + mo + well * c["mo"],
            pair,
            pair,
            slope[2] + c["mg_p"] * dg + c["md_p"] * do + mgd + well * (c["mg"] + c["md"]),
            gas_water,
            rock * bg + c["mg_s"] * dg + gas_water,
        )
        for e in range(9):
            diag_ref[e, i] = out[e].astype(BF16)

    plane_loop(residuals)
    hsend2[0, 0] = first_ref[15]
    hsend2[1, 0] = first_ref[0]
    hsend2[2, 0] = first_ref[:, 15, :]
    hsend2[3, 0] = first_ref[:, 0, :]
    for k in range(4):
        pl.when(neighbour(SIDES[k])[0])(halo_copy(hsend2, hrecv2, k, 1, hs2, hr2).start)
    hi, lo = split(as_rows(first_ref[...]))
    ghl[0:128, :] = hi
    ghl[128:256, :] = lo

    def gather_first(ds):
        for d in ds:

            def store(f, q, value):
                sbuf2[d, pl.ds(q, 1), :] = value

            gather([ghl[...]], 1, row_ref, lane_ref, d, store)
        send_group(sbuf2, rbuf2, ds, fs2, fr2)

    two_groups(gather_first)

    def fault_out(e, carry):
        for di in range(3):
            for q in range(8):
                line = fault_rows[e, pl.ds(di * 24 + q, 3, 8), :]
                fault_ref[e, 0, di, :, pl.ds(q * 128, 128)] = line.astype(BF16)
        return carry

    lax.fori_loop(0, 9, fault_out, 0)
    plane_loop(diagonals)
    wait_halos(hsend2, hrecv2, (1, 1, 1, 1), hs2, hr2)

    def faces(i):
        own = first_ref[i]
        before, after = jnp.maximum(i - 1, 0), jnp.minimum(i + 1, 15)
        up = jnp.where(i == 15, hrecv2[1, 0], first_ref[after])
        down = jnp.where(i == 0, hrecv2[0, 0], first_ref[before])
        total = cond_ref[0, i] * up
        total += jnp.where(i == 0, condlow_ref[0], cond_ref[0, before]) * down
        cj = cond_ref[1, i]
        up = jnp.where(row_id == 15, hrecv2[3, 0, pl.ds(i, 1), :], pltpu.roll(own, 15, 0))
        down = jnp.where(row_id == 0, hrecv2[2, 0, pl.ds(i, 1), :], pltpu.roll(own, 1, 0))
        cj_low = jnp.where(row_id == 0, condlow_ref[1, pl.ds(i, 1), :], pltpu.roll(cj, 1, 0))
        total += cj * up + cj_low * down
        ck = cond_ref[2, i]
        total += ck * pltpu.roll(own, 127, 1) + pltpu.roll(ck * own, 1, 1)
        at = pl.multiple_of(i * 8, 8)
        acc2[pl.ds(at, 8), 0:128] = total[0:8]
        acc2[pl.ds(at, 8), 128:256] = total[8:16]

    plane_loop(faces)
    acc2[128:256, :] = jnp.zeros((128, 256), F32)
    wait_group(sbuf2, rbuf2, group(0), fs2, fr2)
    scatter_first(group(0), row_ref, lane_ref, fcond_ref, rbuf2, acc2)
    wait_group(sbuf2, rbuf2, group(1), fs2, fr2)
    far2[...] = rbuf2[...]


def write_kernel(
    blocks, res_ref, diag_ref, fault_ref, rhs_ref, pd_ref, acc_in, far2, fcond_ref, row_ref, lane_ref,
    face_hbm, res_hbm, diag_hbm, fault_hbm, out_hbm,
    acc2, out_ref, sem,
):
    pairs = ((blocks, face_hbm), (diag_ref, diag_hbm), (res_ref, res_hbm), (fault_ref, fault_hbm), (out_ref, out_hbm))
    copies = [pltpu.make_async_copy(a, b, sem.at[n]) for n, (a, b) in enumerate(pairs)]
    for copy in copies[:4]:
        copy.start()
    acc2[...] = acc_in[...]
    scatter_first((1, 3, 5, 7), row_ref, lane_ref, fcond_ref, far2, acc2)

    def finish(i):
        at = pl.multiple_of(i * 8, 8)
        total = acc2[pl.ds(at, 8), :] + acc2[pl.ds(at + 128, 8), :]
        total = rows([total[:, 0:128], total[:, 128:256]])
        out_ref[i] = (rhs_ref[i] + total) / pd_ref[i]

    plane_loop(finish)
    copies[4].start()
    for copy in copies:
        copy.wait()


def in_vmem(count):
    return [pl.BlockSpec(memory_space=pltpu.VMEM)] * count


def in_hbm(count):
    return [pl.BlockSpec(memory_space=pltpu.HBM)] * count


def per_device(*args):
    p, fc = args[0], args[7]
    slots, cells = fc.shape[3], p.shape

    def placed(n, x):
        if n in (7, 8, 9):
            x = jnp.transpose(x, (1, 2, 0, 3)).reshape(9, 8, 128)
        return pltpu.with_memory_space_constraint(x, pltpu.HBM)

    def f32(*shape):
        return jax.ShapeDtypeStruct(shape, F32)

    def scratch(*shape, dtype=F32):
        return pltpu.VMEM(shape, dtype)

    dma = pltpu.SemaphoreType.DMA
    index = jax.ShapeDtypeStruct((9, 8, 128), jnp.int32)
    face = jax.ShapeDtypeStruct((3, 2, 9) + cells, BF16)
    diag = jax.ShapeDtypeStruct((9,) + cells, BF16)
    fault = jax.ShapeDtypeStruct((9, 1, 3, 3, slots), BF16)
    held = pl.pallas_call(
        system_kernel,
        out_shape=[
            face,
            f32(3, *cells),
            diag,
            fault,
            f32(*cells),
            f32(*cells),
            f32(256, 256),
            f32(9, 8, 128),
            f32(9, 8, 128),
            index,
            index,
        ],
        in_specs=in_hbm(13),
        out_specs=in_vmem(11),
        scratch_shapes=[
            scratch(5, *cells),
            scratch(3, *cells),
            scratch(3, *cells),
            scratch(9, 8, 128, dtype=jnp.int32),
            scratch(9, 8, 128, dtype=jnp.int32),
            scratch(9, 8, 128),
            scratch(1, 128, dtype=jnp.int32),
            scratch(2, 1, 128),
            scratch(9, 4, 8, 128),
            scratch(9, 4, 8, 128),
            scratch(4, 5, 16, 128),
            scratch(4, 5, 16, 128),
            scratch(512, 256, dtype=BF16),
            scratch(512, 256, dtype=BF16),
            scratch(8, 16, 128),
            scratch(8, 16, 128),
            scratch(1024, 256),
            scratch(8, *cells),
            scratch(256, 256),
            scratch(8, 9, 8, 128),
            scratch(9, 72, 128),
            scratch(3, *cells),
            scratch(2, 16, 128),
            scratch(*cells),
            scratch(9, 8, 128),
            scratch(9, 8, 128),
            scratch(4, 1, 16, 128),
            scratch(4, 1, 16, 128),
            scratch(256, 256, dtype=BF16),
            dma((13,)),
            dma((9,)),
            dma((9,)),
            dma((4,)),
            dma((4,)),
            dma((9,)),
            dma((9,)),
            dma((4,)),
            dma((4,)),
        ],
        compiler_params=pltpu.CompilerParams(
            collective_id=0, has_side_effects=True, vmem_limit_bytes=VMEM_BYTES
        ),
        name="system",
    )(*[placed(n, x) for n, x in enumerate(args)])
    face, res, diag, fault, update = pl.pallas_call(
        write_kernel,
        out_shape=[face, f32(3, *cells), diag, fault, f32(*cells)],
        in_specs=in_vmem(11),
        out_specs=in_hbm(5),
        scratch_shapes=[scratch(256, 256), scratch(*cells), dma((5,))],
        compiler_params=pltpu.CompilerParams(vmem_limit_bytes=VMEM_BYTES),
        name="write",
    )(*held)
    return res, diag, face, fault, update


def solution(mesh):
    cells = P("col", "row", None)
    stacked = P(None, "col", "row", None)
    owned = P(("col", "row"), None, None, None)
    wells = P(("col", "row"), None)
    return jax.shard_map(
        per_device,
        mesh=mesh,
        in_specs=(cells,) * 5 + (stacked,) * 2 + (owned,) * 3 + (wells,) * 3,
        out_specs=(
            stacked,
            stacked,
            P(None, None, None, "col", "row", None),
            P(None, ("col", "row"), None, None, None),
            cells,
        ),
        check_vma=False,
    )
```

```python
import jax
import jax.numpy as jnp
from jax import lax
from jax.experimental import pallas as pl
from jax.experimental.pallas import tpu as pltpu
from jax.sharding import PartitionSpec as P

F32 = jnp.float32
BF16 = jnp.bfloat16
F8 = jnp.float8_e4m3fn
LOW = 2.0**-6
MESH = pl.DeviceIdType.MESH
VMEM_BYTES = 40 * 1024 * 1024


def split(x):
    hi = x.astype(BF16)
    return hi, (x - hi.astype(F32)).astype(BF16)


def cell_terms(p, sw, sg):
    oil = 1.0 - sw - sg
    bw = 1.0 + 0.05 * p
    bo = 1.0 + 0.1 * p
    bg = 1.0 + 0.4 * p
    rs = 0.5 + 0.2 * p
    w2 = sw * (sw * (1.0 / 0.3))
    o2 = oil * (oil * (1.0 / 0.8))
    g2 = sg * (sg * (1.0 / 0.05))
    mo = bo * o2
    mo_p = 0.1 * o2
    mo_o = bo * (oil * (2.0 / 0.8))
    return dict(
        mw=bw * w2,
        mo=mo,
        mg=bg * g2,
        md=rs * mo,
        mw_p=0.05 * w2,
        mw_s=bw * (sw * (2.0 / 0.3)),
        mo_p=mo_p,
        mo_o=mo_o,
        mg_p=0.4 * g2,
        mg_s=bg * (sg * (2.0 / 0.05)),
        md_p=0.2 * mo + rs * mo_p,
        md_o=rs * mo_o,
    )


def face_terms(t, a, b, pa, pb, za, zb):
    half = 0.5 * t
    hp = half * (pa - pb)
    hz = half * (za - zb)
    ww = hp - 0.1 * hz
    wo = hp - 0.08 * hz
    wg = hp - 0.02 * hz
    sum_w = a["mw"] + b["mw"]
    sum_o = a["mo"] + b["mo"]
    sum_g = a["mg"] + b["mg"]
    sum_d = a["md"] + b["md"]
    mw = half * sum_w
    mo = half * sum_o
    mgd = half * (sum_g + sum_d)
    flux = (sum_w * ww, sum_o * wo, sum_g * wg + sum_d * wo)
    return (hp, hz, mw, mo, mgd) + flux, (ww, wo, wg)


def block_rows(c, ww, wo, wg, mw, mo, mgd):
    oil = c["mo_o"] * wo
    solved = c["md_o"] * wo
    zero = jnp.zeros_like(ww)
    return (
        c["mw_p"] * ww + mw,
        c["mw_s"] * ww,
        zero,
        c["mo_p"] * wo + mo,
        -oil,
        -oil,
        c["mg_p"] * wg + c["md_p"] * wo + mgd,
        -solved,
        c["mg_s"] * wg - solved,
    )


def neighbour(d):
    a, b = lax.axis_index("col"), lax.axis_index("row")
    ta, tb = a + d // 3 - 1, b + d % 3 - 1
    na, nb = lax.axis_size("col"), lax.axis_size("row")
    there = (ta >= 0) & (ta < na) & (tb >= 0) & (tb < nb)
    return there, (ta, tb)


def direction(g, h, u):
    return jnp.where(g == 0, 2 * u + 6 * h, 4 * h + 2 * u + 1)


def group(g):
    return [direction(g, h, u) for h in range(2) for u in range(2)]


def two_groups(body):
    def step(g, carry):
        body(group(g))
        return carry

    lax.fori_loop(0, 2, step, 0)


SIDES = (7, 1, 5, 3)


def greet():
    barrier = pltpu.get_barrier_semaphore()
    count = 0
    for d in (0, 1, 2, 3, 5, 6, 7, 8):
        there, target = neighbour(d)

        @pl.when(there)
        def _():
            pl.semaphore_signal(barrier, inc=1, device_id=target, device_id_type=MESH)

        count = count + there.astype(jnp.int32)
    return barrier, count


def halo_copy(src, dst, k, count, send_sem, recv_sem):
    return pltpu.make_async_remote_copy(
        src_ref=src.at[k, pl.ds(0, count)],
        dst_ref=dst.at[k, pl.ds(0, count)],
        send_sem=send_sem.at[k],
        recv_sem=recv_sem.at[k],
        device_id=neighbour(SIDES[k])[1],
        device_id_type=MESH,
    )


def fault_copy(src, dst, d, send_sem, recv_sem, back):
    return pltpu.make_async_remote_copy(
        src_ref=src.at[d],
        dst_ref=dst.at[back],
        send_sem=send_sem.at[d],
        recv_sem=recv_sem.at[back],
        device_id=neighbour(d)[1],
        device_id_type=MESH,
    )


def wait_halos(src, dst, counts, send_sem, recv_sem):
    for k in range(4):
        copy = halo_copy(src, dst, k, counts[k], send_sem, recv_sem)
        pl.when(neighbour(SIDES[k])[0])(copy.wait_send)
        pl.when(neighbour(8 - SIDES[k])[0])(copy.wait_recv)


def send_group(src, dst, ds, send_sem, recv_sem):
    for d in ds:
        pl.when(neighbour(d)[0])(fault_copy(src, dst, d, send_sem, recv_sem, 8 - d).start)


def wait_group(src, dst, ds, send_sem, recv_sem):
    for d in ds:
        copy = fault_copy(src, dst, d, send_sem, recv_sem, d)

        @pl.when(neighbour(d)[0])
        def _():
            copy.wait_send()
            copy.wait_recv()


def clear_missing(hrecv, rbuf):
    for k in range(4):

        @pl.when(jnp.logical_not(neighbour(8 - SIDES[k])[0]))
        def _():
            hrecv[k] = jnp.zeros_like(hrecv[k])

    def one(d, carry):
        @pl.when(jnp.logical_not(neighbour(d)[0]) | (d == 4))
        def _():
            rbuf[d] = jnp.zeros_like(rbuf[d])

        return carry

    lax.fori_loop(0, 9, one, 0)


def cell_rows(column, layer):
    return (column >> 4) * 8 + (column & 7), ((column >> 3) & 1) * 128 + layer


def hot(index, size):
    slots = index.shape[1]
    row = jnp.broadcast_to(index.astype(F32), (16, slots)).astype(BF16)
    iota = lax.broadcasted_iota(jnp.int32, (size, slots), 0).astype(F32).astype(BF16)
    return iota.reshape(size // 16, 16, slots) == row[None]


def hot_values(mask, value_row):
    slots = value_row.shape[1]
    hi, lo = split(jnp.broadcast_to(value_row, (16, slots)))
    zero = jnp.zeros((), BF16)
    return [jnp.where(mask, v[None], zero).reshape(128, slots) for v in (hi, lo)]


def hot_low_values(mask, value_row):
    slots = value_row.shape[1]
    value = jnp.broadcast_to(value_row, (16, slots))
    hi = value.astype(BF16)
    lo = ((value - hi.astype(F32)) * (1.0 / LOW)).astype(BF16)
    zero = jnp.zeros((), BF16)
    return [jnp.where(mask, v[None], zero).reshape(128, slots) for v in (hi, lo)]


def hot_ones(mask):
    size = mask.shape[0] * 16
    return jnp.where(mask, jnp.ones((), BF16), jnp.zeros((), BF16)).reshape(size, mask.shape[2])


def lanes(parts):
    return jnp.concatenate(parts, axis=1)


def rows(parts):
    return jnp.concatenate(parts, axis=0)


def as_rows(x):
    return lanes([x[:, 0:8, :].reshape(128, 128), x[:, 8:16, :].reshape(128, 128)])


def dot_slots(weighted, put):
    return lax.dot_general(weighted, put, (((1,), (1,)), ((), ())), preferred_element_type=F32)


def gather(pieces, count, row_ref, lane_ref, d, store):
    for c in range(0, 8, 2):
        pick = lanes([hot_ones(hot(lane_ref[d, pl.ds(q, 1), :], 256)) for q in (c, c + 1)])
        lines = None
        for piece in pieces:
            line = jnp.dot(piece, pick, preferred_element_type=F32)
            lines = line if lines is None else lines + line
        for s in range(2):
            mask = lax.broadcasted_iota(jnp.int32, (128, 128), 0) == row_ref[d, pl.ds(c + s, 1), :]
            for f in range(count):
                part = lines[f * 128 : (f + 1) * 128, s * 128 : (s + 1) * 128]
                if len(pieces) == 1:
                    at = (count + f) * 128
                    part = part + lines[at : at + 128, s * 128 : (s + 1) * 128]
                store(f, c + s, jnp.sum(jnp.where(mask, part, 0.0), axis=0, keepdims=True))


def lower_side(values):
    return (-values[0], -values[1], values[2], values[3], values[4]) + tuple(-v for v in values[5:])


def plane_loop(body):
    def step(i, carry):
        body(2 * i)
        body(2 * i + 1)
        return carry

    lax.fori_loop(0, 8, step, 0)


def rows_of(ref, start):
    at = pl.multiple_of(start, 8)
    return rows([ref[pl.ds(at, 8), 0:128], ref[pl.ds(at, 8), 128:256]])


def scatter_first(ds, row_ref, lane_ref, fcond_ref, far_ref, acc2):
    for d in ds:
        values = fcond_ref[d] * far_ref[d]
        for c in range(0, 8, 2):
            pair = (c, c + 1)
            put = lanes([hot_ones(hot(lane_ref[d, pl.ds(q, 1), :], 256)) for q in pair])
            both = [hot_values(hot(row_ref[d, pl.ds(q, 1), :], 128), values[q : q + 1]) for q in pair]
            weighted = rows([lanes([x[0] for x in both]), lanes([x[1] for x in both])])
            acc2[...] += dot_slots(weighted, put)


def system_kernel(
    p_hbm, sw_hbm, sg_hbm, z_hbm, pv_hbm, om_hbm, t_hbm, fc_hbm, fl_hbm, ft_hbm, pc_hbm, wi_hbm, wp_hbm,
    blocks, res_ref, diag_ref, fault_ref, rhs_ref, pd_ref, acc2, far2, fcond_ref, row_ref, lane_ref,
    x_ref, t_ref, om_ref, fc_ref, fl_ref, ft_ref, pc_ref, w_ref, sbuf, rbuf, hsend, hrecv, ghi, glo, lowj,
    carry_ref, acc, fa, wacc, chan, fault_rows, cond_ref, condlow_ref, first_ref, sbuf2, rbuf2, hsend2, hrecv2, ghl,
    in_sem, fs, fr, hs, hr, fs2, fr2, hs2, hr2,
):
    barrier, count = greet()
    pairs = [(fc_hbm, fc_ref), (fl_hbm, fl_ref)]
    pairs += [(ref, x_ref.at[f]) for f, ref in enumerate((p_hbm, sw_hbm, sg_hbm, z_hbm))]
    pairs += [(t_hbm, t_ref), (ft_hbm, ft_ref), (pc_hbm, pc_ref), (wi_hbm, w_ref.at[0]), (wp_hbm, w_ref.at[1])]
    pairs += [(pv_hbm, x_ref.at[4]), (om_hbm, om_ref)]
    loads = [pltpu.make_async_copy(a, b, in_sem.at[n]) for n, (a, b) in enumerate(pairs)]
    for load in loads:
        load.start()
    clear_missing(hrecv, rbuf)
    clear_missing(hrecv2, rbuf2)
    fault_rows[:, 32:40, :] = jnp.zeros((9, 8, 128), F32)
    fcond_ref[4] = jnp.zeros((8, 128), F32)
    acc[...] = jnp.zeros_like(acc)
    for load in loads[:2]:
        load.wait()
    row, lane = cell_rows(fc_ref[...], fl_ref[...])
    row_ref[...] = row
    lane_ref[...] = lane
    for load in loads[2:6]:
        load.wait()
    for f in range(4):
        hi, lo = split(as_rows(x_ref[f]))
        ghi[pl.ds(f * 128, 128), :] = hi
        glo[pl.ds(f * 128, 128), :] = lo
    counts = (5, 4, 5, 4)

    def gather_four(ds):
        for d in ds:

            def store(f, q, value):
                sbuf[d, f, pl.ds(q, 1), :] = value

            gather([ghi[...], glo[...]], 4, row_ref, lane_ref, d, store)

    gather_four((0, 2, 6, 8))
    for f in range(4):
        hsend[0, f] = x_ref[f, 15]
        hsend[1, f] = x_ref[f, 0]
        hsend[2, f] = x_ref[f, :, 15, :]
        hsend[3, f] = x_ref[f, :, 0, :]
    loads[6].wait()
    hsend[0, 4] = t_ref[0, 15]
    hsend[2, 4] = t_ref[1, :, 15, :]
    pl.semaphore_wait(barrier, count)
    for k in range(4):
        pl.when(neighbour(SIDES[k])[0])(halo_copy(hsend, hrecv, k, counts[k], hs, hr).start)
    send_group(sbuf, rbuf, (0, 2, 6, 8), fs, fr)
    gather_four((1, 3, 5, 7))
    send_group(sbuf, rbuf, (1, 3, 5, 7), fs, fr)
    for load in loads[7:]:
        load.wait()
    wait_halos(hsend, hrecv, counts, hs, hr)

    def low_face(k, fields):
        a = [hrecv[k, f] for f in range(4)]
        values, _ = face_terms(
            hrecv[k, 4], cell_terms(*a[:3]), cell_terms(*fields[:3]), a[0], fields[0], a[3], fields[3]
        )
        condlow_ref[k // 2] = values[2] + values[3] + values[4]
        return lower_side(values)

    for v, value in enumerate(low_face(2, [x_ref[f, :, 0, :] for f in range(4)])):
        lowj[v] = value
    for v, value in enumerate(low_face(0, [x_ref[f, 0] for f in range(4)])):
        carry_ref[v] = value
    row_id = lax.broadcasted_iota(jnp.int32, (16, 128), 0)
    lane_id = lax.broadcasted_iota(jnp.int32, (16, 128), 1)
    keep_i = jnp.where(neighbour(SIDES[0])[0], 1.0, 0.0)
    keep_j = jnp.where(neighbour(SIDES[2])[0], 1.0, 0.0)

    def plane(i, carry):
        own = [x_ref[f, i] for f in range(4)]
        a = cell_terms(*own[:3])
        last = i == 15
        after = jnp.minimum(i + 1, 15)
        total = list(carry)
        out_carry = None
        for n in range(3):
            t = t_ref[n, i]
            if n == 0:
                nxt = [jnp.where(last, hrecv[1, f], x_ref[f, after]) for f in range(4)]
                t = t * jnp.where(last, keep_i, 1.0)
            elif n == 1:
                nxt = [
                    jnp.where(row_id == 15, hrecv[3, f, pl.ds(i, 1), :], pltpu.roll(own[f], 15, 0))
                    for f in range(4)
                ]
                t = jnp.where(row_id == 15, t * keep_j, t)
            else:
                nxt = [pltpu.roll(own[f], 127, 1) for f in range(4)]
                t = jnp.where(lane_id == 127, 0.0, t)
            b = cell_terms(*nxt[:3])
            values, (ww, wo, wg) = face_terms(t, a, b, own[0], nxt[0], own[3], nxt[3])
            mw, mo, mgd = values[2:5]
            cond_ref[n, i] = mw + mo + mgd
            upper = block_rows(b, ww, wo, wg, -mw, -mo, -mgd)
            lower = block_rows(a, -ww, -wo, -wg, -mw, -mo, -mgd)
            for e in range(9):
                blocks[n, 0, e, i] = upper[e].astype(BF16)
                blocks[n, 1, e, i] = lower[e].astype(BF16)
            total = [x + y for x, y in zip(total, values)]
            below = lower_side(values)
            if n == 0:
                out_carry = below
            elif n == 1:
                for v in range(8):
                    shifted = jnp.where(row_id == 0, lowj[v, pl.ds(i, 1), :], pltpu.roll(below[v], 1, 0))
                    total[v] = total[v] + shifted
            else:
                total = [x + pltpu.roll(y, 1, 1) for x, y in zip(total, below)]
        for v in range(8):
            fa[v, i] = total[v]
        return out_carry

    def fault_terms(d):
        near = [sbuf[d, f] for f in range(4)]
        far = [rbuf[d, f] for f in range(4)]
        a, b = cell_terms(*near[:3]), cell_terms(*far[:3])
        values, (ww, wo, wg) = face_terms(ft_ref[d], a, b, near[0], far[0], near[3], far[3])
        mw, mo, mgd = values[2:5]
        fcond_ref[d] = mw + mo + mgd
        for v in range(8):
            chan[v, d] = values[v]
        for e, value in enumerate(block_rows(b, ww, wo, wg, -mw, -mo, -mgd)):
            fault_rows[e, pl.ds(pl.multiple_of(d * 8, 8), 8), :] = value

    def scatter(d, c):
        four = range(c, c + 4)
        put = lanes([hot_ones(hot(lane_ref[d, pl.ds(q, 1), :], 256)) for q in four])
        masks = [hot(row_ref[d, pl.ds(q, 1), :], 128) for q in four]
        his, los = [], []
        for v in range(8):
            both = [hot_low_values(m, chan[v, d, pl.ds(q, 1), :]) for m, q in zip(masks, four)]
            his.append(lanes([x[0] for x in both]))
            los.append(lanes([x[1] for x in both]))
        low_put = (put * jnp.asarray(LOW, BF16)).astype(F8)
        acc[...] += dot_slots(rows(his), put) + dot_slots(rows(los).astype(F8), low_put)

    def main_group(g, carry):
        wait_group(sbuf, rbuf, group(g), fs, fr)
        for d in group(g):
            fault_terms(d)

        def half(h, carry):
            below = [carry_ref[v] for v in range(8)]
            for u in range(2):
                for m in range(2):
                    scatter(direction(g, h, u), 4 * m)
                    below = plane(g * 8 + h * 4 + u * 2 + m, below)
            for v in range(8):
                carry_ref[v] = below[v]
            return carry

        lax.fori_loop(0, 2, half, 0)
        return carry

    lax.fori_loop(0, 2, main_group, 0)

    cell = pc_ref[...]
    row, lane = cell_rows(cell >> 7, cell & 127)
    mask = hot(row, 128)
    hi_w, lo_w = hot_values(mask, w_ref[0])
    hi_q, lo_q = hot_values(mask, w_ref[0] * w_ref[1])
    put = hot_ones(hot(lane, 256))
    wacc[...] = dot_slots(lanes([rows([hi_w, hi_q]), rows([lo_w, lo_q])]), lanes([put, put]))

    def sums(i):
        return [fa[v, i] + rows_of(acc, v * 128 + i * 8) for v in range(8)]

    def accumulation(i):
        p, sw, sg = x_ref[0, i], x_ref[1, i], x_ref[2, i]
        well = rows_of(wacc, i * 8)
        drive = rows_of(wacc, 128 + i * 8) - p * well
        oil = 1.0 - sw - sg
        pv = x_ref[4, i]
        rock = 2.0 * (pv * (1.0 + 0.02 * p))
        rock_p = 0.04 * pv
        bw, bo, bg, rs = 1.0 + 0.05 * p, 1.0 + 0.1 * p, 1.0 + 0.4 * p, 0.5 + 0.2 * p
        ob = oil * bo
        gas = sg * bg + rs * ob
        a0 = rock_p * sw * bw + rock * sw * 0.05
        a3 = rock_p * ob + rock * oil * 0.1
        a6 = rock_p * gas + rock * (0.4 * sg + 0.2 * ob + 0.1 * rs * oil)
        return cell_terms(p, sw, sg), well, drive, rock, (rock * sw * bw, rock * ob, rock * gas), (a0, a3, a6), (bw, bo, bg, rs)

    def residuals(i):
        _, _, mw, mo, mgd, rw, ro, rg = sums(i)
        c, well, drive, rock, held, slope, _ = accumulation(i)
        r0 = held[0] - 2.0 * om_ref[0, i] + rw - drive * c["mw"]
        r1 = held[1] - 2.0 * om_ref[1, i] + ro - drive * c["mo"]
        r2 = held[2] - 2.0 * om_ref[2, i] + rg - drive * (c["mg"] + c["md"])
        res_ref[0, i], res_ref[1, i], res_ref[2, i] = r0, r1, r2
        total = c["mw"] + c["mo"] + c["mg"] + c["md"]
        pd = slope[0] + slope[1] + slope[2] + mw + mo + mgd + well * total
        rhs = -(r0 + r1 + r2)
        rhs_ref[i] = rhs
        pd_ref[i] = pd
        first_ref[i] = rhs / pd

    def diagonals(i):
        hp, hz, mw, mo, mgd, _, _, _ = sums(i)
        c, well, drive, rock, held, slope, (bw, bo, bg, rs) = accumulation(i)
        dw = hp - 0.1 * hz - drive
        do = hp - 0.08 * hz - drive
        dg = hp - 0.02 * hz - drive
        pair = -(rock * bo) - c["mo_o"] * do
        gas_water = -(rock * rs * bo) - c["md_o"] * do
        out = (
            slope[0] + c["mw_p"] * dw + mw + well * c["mw"],
            rock * bw + c["mw_s"] * dw,
            jnp.zeros_like(dw),
            slope[1] + c["mo_p"] * do + mo + well * c["mo"],
            pair,
            pair,
            slope[2] + c["mg_p"] * dg + c["md_p"] * do + mgd + well * (c["mg"] + c["md"]),
            gas_water,
            rock * bg + c["mg_s"] * dg + gas_water,
        )
        for e in range(9):
            diag_ref[e, i] = out[e].astype(BF16)

    plane_loop(residuals)
    hsend2[0, 0] = first_ref[15]
    hsend2[1, 0] = first_ref[0]
    hsend2[2, 0] = first_ref[:, 15, :]
    hsend2[3, 0] = first_ref[:, 0, :]
    for k in range(4):
        pl.when(neighbour(SIDES[k])[0])(halo_copy(hsend2, hrecv2, k, 1, hs2, hr2).start)
    hi, lo = split(as_rows(first_ref[...]))
    ghl[0:128, :] = hi
    ghl[128:256, :] = lo

    def gather_first(ds):
        for d in ds:

            def store(f, q, value):
                sbuf2[d, pl.ds(q, 1), :] = value

            gather([ghl[...]], 1, row_ref, lane_ref, d, store)
        send_group(sbuf2, rbuf2, ds, fs2, fr2)

    two_groups(gather_first)

    def fault_out(e, carry):
        for di in range(3):
            for q in range(8):
                line = fault_rows[e, pl.ds(di * 24 + q, 3, 8), :]
                fault_ref[e, 0, di, :, pl.ds(q * 128, 128)] = line.astype(BF16)
        return carry

    lax.fori_loop(0, 9, fault_out, 0)
    plane_loop(diagonals)
    wait_halos(hsend2, hrecv2, (1, 1, 1, 1), hs2, hr2)

    def faces(i):
        own = first_ref[i]
        before, after = jnp.maximum(i - 1, 0), jnp.minimum(i + 1, 15)
        up = jnp.where(i == 15, hrecv2[1, 0], first_ref[after])
        down = jnp.where(i == 0, hrecv2[0, 0], first_ref[before])
        total = cond_ref[0, i] * up
        total += jnp.where(i == 0, condlow_ref[0], cond_ref[0, before]) * down
        cj = cond_ref[1, i]
        up = jnp.where(row_id == 15, hrecv2[3, 0, pl.ds(i, 1), :], pltpu.roll(own, 15, 0))
        down = jnp.where(row_id == 0, hrecv2[2, 0, pl.ds(i, 1), :], pltpu.roll(own, 1, 0))
        cj_low = jnp.where(row_id == 0, condlow_ref[1, pl.ds(i, 1), :], pltpu.roll(cj, 1, 0))
        total += cj * up + cj_low * down
        ck = cond_ref[2, i]
        total += ck * pltpu.roll(own, 127, 1) + pltpu.roll(ck * own, 1, 1)
        at = pl.multiple_of(i * 8, 8)
        acc2[pl.ds(at, 8), 0:128] = total[0:8]
        acc2[pl.ds(at, 8), 128:256] = total[8:16]

    plane_loop(faces)
    acc2[128:256, :] = jnp.zeros((128, 256), F32)
    wait_group(sbuf2, rbuf2, group(0), fs2, fr2)
    scatter_first(group(0), row_ref, lane_ref, fcond_ref, rbuf2, acc2)
    wait_group(sbuf2, rbuf2, group(1), fs2, fr2)
    far2[...] = rbuf2[...]


def write_kernel(
    blocks, res_ref, diag_ref, fault_ref, rhs_ref, pd_ref, acc_in, far2, fcond_ref, row_ref, lane_ref,
    face_hbm, res_hbm, diag_hbm, fault_hbm, out_hbm,
    acc2, out_ref, sem,
):
    pairs = ((blocks, face_hbm), (diag_ref, diag_hbm), (res_ref, res_hbm), (fault_ref, fault_hbm), (out_ref, out_hbm))
    copies = [pltpu.make_async_copy(a, b, sem.at[n]) for n, (a, b) in enumerate(pairs)]
    for copy in copies[:4]:
        copy.start()
    acc2[...] = acc_in[...]
    scatter_first((1, 3, 5, 7), row_ref, lane_ref, fcond_ref, far2, acc2)

    def finish(i):
        at = pl.multiple_of(i * 8, 8)
        total = acc2[pl.ds(at, 8), :] + acc2[pl.ds(at + 128, 8), :]
        total = rows([total[:, 0:128], total[:, 128:256]])
        out_ref[i] = (rhs_ref[i] + total) / pd_ref[i]

    plane_loop(finish)
    copies[4].start()
    for copy in copies:
        copy.wait()


def in_vmem(count):
    return [pl.BlockSpec(memory_space=pltpu.VMEM)] * count


def in_hbm(count):
    return [pl.BlockSpec(memory_space=pltpu.HBM)] * count


def per_device(*args):
    p, fc = args[0], args[7]
    slots, cells = fc.shape[3], p.shape

    def placed(n, x):
        if n in (7, 8, 9):
            x = jnp.transpose(x, (1, 2, 0, 3)).reshape(9, 8, 128)
        return pltpu.with_memory_space_constraint(x, pltpu.HBM)

    def f32(*shape):
        return jax.ShapeDtypeStruct(shape, F32)

    def scratch(*shape, dtype=F32):
        return pltpu.VMEM(shape, dtype)

    dma = pltpu.SemaphoreType.DMA
    index = jax.ShapeDtypeStruct((9, 8, 128), jnp.int32)
    face = jax.ShapeDtypeStruct((3, 2, 9) + cells, BF16)
    diag = jax.ShapeDtypeStruct((9,) + cells, BF16)
    fault = jax.ShapeDtypeStruct((9, 1, 3, 3, slots), BF16)
    held = pl.pallas_call(
        system_kernel,
        out_shape=[
            face,
            f32(3, *cells),
            diag,
            fault,
            f32(*cells),
            f32(*cells),
            f32(256, 256),
            f32(9, 8, 128),
            f32(9, 8, 128),
            index,
            index,
        ],
        in_specs=in_hbm(13),
        out_specs=in_vmem(11),
        scratch_shapes=[
            scratch(5, *cells),
            scratch(3, *cells),
            scratch(3, *cells),
            scratch(9, 8, 128, dtype=jnp.int32),
            scratch(9, 8, 128, dtype=jnp.int32),
            scratch(9, 8, 128),
            scratch(1, 128, dtype=jnp.int32),
            scratch(2, 1, 128),
            scratch(9, 4, 8, 128),
            scratch(9, 4, 8, 128),
            scratch(4, 5, 16, 128),
            scratch(4, 5, 16, 128),
            scratch(512, 256, dtype=BF16),
            scratch(512, 256, dtype=BF16),
            scratch(8, 16, 128),
            scratch(8, 16, 128),
            scratch(1024, 256),
            scratch(8, *cells),
            scratch(256, 256),
            scratch(8, 9, 8, 128),
            scratch(9, 72, 128),
            scratch(3, *cells),
            scratch(2, 16, 128),
            scratch(*cells),
            scratch(9, 8, 128),
            scratch(9, 8, 128),
            scratch(4, 1, 16, 128),
            scratch(4, 1, 16, 128),
            scratch(256, 256, dtype=BF16),
            dma((13,)),
            dma((9,)),
            dma((9,)),
            dma((4,)),
            dma((4,)),
            dma((9,)),
            dma((9,)),
            dma((4,)),
            dma((4,)),
        ],
        compiler_params=pltpu.CompilerParams(
            collective_id=0, has_side_effects=True, vmem_limit_bytes=VMEM_BYTES
        ),
        name="system",
    )(*[placed(n, x) for n, x in enumerate(args)])
    face, res, diag, fault, update = pl.pallas_call(
        write_kernel,
        out_shape=[face, f32(3, *cells), diag, fault, f32(*cells)],
        in_specs=in_vmem(11),
        out_specs=in_hbm(5),
        scratch_shapes=[scratch(256, 256), scratch(*cells), dma((5,))],
        compiler_params=pltpu.CompilerParams(vmem_limit_bytes=VMEM_BYTES),
        name="write",
    )(*held)
    return res, diag, face, fault, update


def solution(mesh):
    cells = P("col", "row", None)
    stacked = P(None, "col", "row", None)
    owned = P(("col", "row"), None, None, None)
    wells = P(("col", "row"), None)
    return jax.shard_map(
        per_device,
        mesh=mesh,
        in_specs=(cells,) * 5 + (stacked,) * 2 + (owned,) * 3 + (wells,) * 3,
        out_specs=(
            stacked,
            stacked,
            P(None, None, None, "col", "row", None),
            P(None, ("col", "row"), None, None, None),
            cells,
        ),
        check_vma=False,
    )
```

```python
import jax
import jax.numpy as jnp
from jax import lax
from jax.experimental import pallas as pl
from jax.experimental.pallas import tpu as pltpu
from jax.sharding import PartitionSpec as P

F32 = jnp.float32
BF16 = jnp.bfloat16
F8 = jnp.float8_e4m3fn
LOW = 2.0**-6
MESH = pl.DeviceIdType.MESH
VMEM_BYTES = 40 * 1024 * 1024


def split(x):
    hi = x.astype(BF16)
    return hi, (x - hi.astype(F32)).astype(BF16)


def cell_terms(p, sw, sg):
    oil = 1.0 - sw - sg
    bw = 1.0 + 0.05 * p
    bo = 1.0 + 0.1 * p
    bg = 1.0 + 0.4 * p
    rs = 0.5 + 0.2 * p
    w2 = sw * (sw * (1.0 / 0.3))
    o2 = oil * (oil * (1.0 / 0.8))
    g2 = sg * (sg * (1.0 / 0.05))
    mo = bo * o2
    mo_p = 0.1 * o2
    mo_o = bo * (oil * (2.0 / 0.8))
    return dict(
        mw=bw * w2,
        mo=mo,
        mg=bg * g2,
        md=rs * mo,
        mw_p=0.05 * w2,
        mw_s=bw * (sw * (2.0 / 0.3)),
        mo_p=mo_p,
        mo_o=mo_o,
        mg_p=0.4 * g2,
        mg_s=bg * (sg * (2.0 / 0.05)),
        md_p=0.2 * mo + rs * mo_p,
        md_o=rs * mo_o,
    )


def face_terms(t, a, b, pa, pb, za, zb):
    half = 0.5 * t
    hp = half * (pa - pb)
    hz = half * (za - zb)
    ww = hp - 0.1 * hz
    wo = hp - 0.08 * hz
    wg = hp - 0.02 * hz
    sum_w = a["mw"] + b["mw"]
    sum_o = a["mo"] + b["mo"]
    sum_g = a["mg"] + b["mg"]
    sum_d = a["md"] + b["md"]
    mw = half * sum_w
    mo = half * sum_o
    mgd = half * (sum_g + sum_d)
    flux = (sum_w * ww, sum_o * wo, sum_g * wg + sum_d * wo)
    return (hp, hz, mw, mo, mgd) + flux, (ww, wo, wg)


def block_rows(c, ww, wo, wg, mw, mo, mgd):
    oil = c["mo_o"] * wo
    solved = c["md_o"] * wo
    zero = jnp.zeros_like(ww)
    return (
        c["mw_p"] * ww + mw,
        c["mw_s"] * ww,
        zero,
        c["mo_p"] * wo + mo,
        -oil,
        -oil,
        c["mg_p"] * wg + c["md_p"] * wo + mgd,
        -solved,
        c["mg_s"] * wg - solved,
    )


def neighbour(d):
    a, b = lax.axis_index("col"), lax.axis_index("row")
    ta, tb = a + d // 3 - 1, b + d % 3 - 1
    na, nb = lax.axis_size("col"), lax.axis_size("row")
    there = (ta >= 0) & (ta < na) & (tb >= 0) & (tb < nb)
    return there, (ta, tb)


def direction(g, h, u):
    return jnp.where(g == 0, 2 * u + 6 * h, 4 * h + 2 * u + 1)


def group(g):
    return [direction(g, h, u) for h in range(2) for u in range(2)]


def two_groups(body):
    def step(g, carry):
        body(group(g))
        return carry

    lax.fori_loop(0, 2, step, 0)


SIDES = (7, 1, 5, 3)


def greet():
    barrier = pltpu.get_barrier_semaphore()
    count = 0
    for d in (0, 1, 2, 3, 5, 6, 7, 8):
        there, target = neighbour(d)

        @pl.when(there)
        def _():
            pl.semaphore_signal(barrier, inc=1, device_id=target, device_id_type=MESH)

        count = count + there.astype(jnp.int32)
    return barrier, count


def halo_copy(src, dst, k, count, send_sem, recv_sem):
    return pltpu.make_async_remote_copy(
        src_ref=src.at[k, pl.ds(0, count)],
        dst_ref=dst.at[k, pl.ds(0, count)],
        send_sem=send_sem.at[k],
        recv_sem=recv_sem.at[k],
        device_id=neighbour(SIDES[k])[1],
        device_id_type=MESH,
    )


def fault_copy(src, dst, d, send_sem, recv_sem, back):
    return pltpu.make_async_remote_copy(
        src_ref=src.at[d],
        dst_ref=dst.at[back],
        send_sem=send_sem.at[d],
        recv_sem=recv_sem.at[back],
        device_id=neighbour(d)[1],
        device_id_type=MESH,
    )


def wait_halos(src, dst, counts, send_sem, recv_sem):
    for k in range(4):
        copy = halo_copy(src, dst, k, counts[k], send_sem, recv_sem)
        pl.when(neighbour(SIDES[k])[0])(copy.wait_send)
        pl.when(neighbour(8 - SIDES[k])[0])(copy.wait_recv)


def send_group(src, dst, ds, send_sem, recv_sem):
    for d in ds:
        pl.when(neighbour(d)[0])(fault_copy(src, dst, d, send_sem, recv_sem, 8 - d).start)


def wait_group(src, dst, ds, send_sem, recv_sem):
    for d in ds:
        copy = fault_copy(src, dst, d, send_sem, recv_sem, d)

        @pl.when(neighbour(d)[0])
        def _():
            copy.wait_send()
            copy.wait_recv()


def clear_missing(hrecv, rbuf):
    for k in range(4):

        @pl.when(jnp.logical_not(neighbour(8 - SIDES[k])[0]))
        def _():
            hrecv[k] = jnp.zeros_like(hrecv[k])

    def one(d, carry):
        @pl.when(jnp.logical_not(neighbour(d)[0]) | (d == 4))
        def _():
            rbuf[d] = jnp.zeros_like(rbuf[d])

        return carry

    lax.fori_loop(0, 9, one, 0)


def cell_rows(column, layer):
    return (column >> 4) * 8 + (column & 7), ((column >> 3) & 1) * 128 + layer


def hot(index, size):
    slots = index.shape[1]
    row = jnp.broadcast_to(index.astype(F32), (16, slots)).astype(BF16)
    iota = lax.broadcasted_iota(jnp.int32, (size, slots), 0).astype(F32).astype(BF16)
    return iota.reshape(size // 16, 16, slots) == row[None]


def hot_values(mask, value_row):
    slots = value_row.shape[1]
    hi, lo = split(jnp.broadcast_to(value_row, (16, slots)))
    zero = jnp.zeros((), BF16)
    return [jnp.where(mask, v[None], zero).reshape(128, slots) for v in (hi, lo)]


def hot_low_values(mask, value_row):
    slots = value_row.shape[1]
    value = jnp.broadcast_to(value_row, (16, slots))
    hi = value.astype(BF16)
    lo = ((value - hi.astype(F32)) * (1.0 / LOW)).astype(BF16)
    zero = jnp.zeros((), BF16)
    return [jnp.where(mask, v[None], zero).reshape(128, slots) for v in (hi, lo)]


def hot_ones(mask):
    size = mask.shape[0] * 16
    return jnp.where(mask, jnp.ones((), BF16), jnp.zeros((), BF16)).reshape(size, mask.shape[2])


def lanes(parts):
    return jnp.concatenate(parts, axis=1)


def rows(parts):
    return jnp.concatenate(parts, axis=0)


def as_rows(x):
    return lanes([x[:, 0:8, :].reshape(128, 128), x[:, 8:16, :].reshape(128, 128)])


def dot_slots(weighted, put):
    return lax.dot_general(weighted, put, (((1,), (1,)), ((), ())), preferred_element_type=F32)


def gather(pieces, count, row_ref, lane_ref, d, store):
    for c in range(0, 8, 2):
        pick = lanes([hot_ones(hot(lane_ref[d, pl.ds(q, 1), :], 256)) for q in (c, c + 1)])
        lines = None
        for piece in pieces:
            line = jnp.dot(piece, pick, preferred_element_type=F32)
            lines = line if lines is None else lines + line
        for s in range(2):
            mask = lax.broadcasted_iota(jnp.int32, (128, 128), 0) == row_ref[d, pl.ds(c + s, 1), :]
            for f in range(count):
                part = lines[f * 128 : (f + 1) * 128, s * 128 : (s + 1) * 128]
                if len(pieces) == 1:
                    at = (count + f) * 128
                    part = part + lines[at : at + 128, s * 128 : (s + 1) * 128]
                store(f, c + s, jnp.sum(jnp.where(mask, part, 0.0), axis=0, keepdims=True))


def lower_side(values):
    return (-values[0], -values[1], values[2], values[3], values[4]) + tuple(-v for v in values[5:])


def plane_loop(body):
    def step(i, carry):
        body(2 * i)
        body(2 * i + 1)
        return carry

    lax.fori_loop(0, 8, step, 0)


def rows_of(ref, start):
    at = pl.multiple_of(start, 8)
    return rows([ref[pl.ds(at, 8), 0:128], ref[pl.ds(at, 8), 128:256]])


def scatter_first(ds, row_ref, lane_ref, fcond_ref, far_ref, acc2):
    for d in ds:
        values = fcond_ref[d] * far_ref[d]
        for c in range(0, 8, 2):
            pair = (c, c + 1)
            put = lanes([hot_ones(hot(lane_ref[d, pl.ds(q, 1), :], 256)) for q in pair])
            both = [hot_values(hot(row_ref[d, pl.ds(q, 1), :], 128), values[q : q + 1]) for q in pair]
            weighted = rows([lanes([x[0] for x in both]), lanes([x[1] for x in both])])
            acc2[...] += dot_slots(weighted, put)


def system_kernel(
    p_hbm, sw_hbm, sg_hbm, z_hbm, pv_hbm, om_hbm, t_hbm, fc_hbm, fl_hbm, ft_hbm, pc_hbm, wi_hbm, wp_hbm,
    blocks, res_ref, diag_ref, fault_ref, rhs_ref, pd_ref, acc2, far2, fcond_ref, row_ref, lane_ref,
    x_ref, t_ref, om_ref, fc_ref, fl_ref, ft_ref, pc_ref, w_ref, sbuf, rbuf, hsend, hrecv, ghi, glo, lowj,
    carry_ref, acc, fa, wacc, chan, fault_rows, cond_ref, condlow_ref, first_ref, sbuf2, rbuf2, hsend2, hrecv2, ghl,
    in_sem, fs, fr, hs, hr, fs2, fr2, hs2, hr2,
):
    barrier, count = greet()
    pairs = [(fc_hbm, fc_ref), (fl_hbm, fl_ref)]
    pairs += [(ref, x_ref.at[f]) for f, ref in enumerate((p_hbm, sw_hbm, sg_hbm, z_hbm))]
    pairs += [(t_hbm, t_ref), (ft_hbm, ft_ref), (pc_hbm, pc_ref), (wi_hbm, w_ref.at[0]), (wp_hbm, w_ref.at[1])]
    pairs += [(pv_hbm, x_ref.at[4]), (om_hbm, om_ref)]
    loads = [pltpu.make_async_copy(a, b, in_sem.at[n]) for n, (a, b) in enumerate(pairs)]
    for load in loads:
        load.start()
    clear_missing(hrecv, rbuf)
    clear_missing(hrecv2, rbuf2)
    fault_rows[:, 32:40, :] = jnp.zeros((9, 8, 128), F32)
    fcond_ref[4] = jnp.zeros((8, 128), F32)
    acc[...] = jnp.zeros_like(acc)
    for load in loads[:2]:
        load.wait()
    row, lane = cell_rows(fc_ref[...], fl_ref[...])
    row_ref[...] = row
    lane_ref[...] = lane
    for load in loads[2:6]:
        load.wait()
    for f in range(4):
        hi, lo = split(as_rows(x_ref[f]))
        ghi[pl.ds(f * 128, 128), :] = hi
        glo[pl.ds(f * 128, 128), :] = lo
    counts = (5, 4, 5, 4)

    def gather_some(ds):
        for d in ds:

            def store(f, q, value):
                sbuf[d, f, pl.ds(q, 1), :] = value

            gather([ghi[...], glo[...]], 4, row_ref, lane_ref, d, store)

    gather_some((0, 2))
    for f in range(4):
        hsend[0, f] = x_ref[f, 15]
        hsend[1, f] = x_ref[f, 0]
        hsend[2, f] = x_ref[f, :, 15, :]
        hsend[3, f] = x_ref[f, :, 0, :]
    loads[6].wait()
    hsend[0, 4] = t_ref[0, 15]
    hsend[2, 4] = t_ref[1, :, 15, :]
    pl.semaphore_wait(barrier, count)
    for k in (2, 3, 0, 1):
        pl.when(neighbour(SIDES[k])[0])(halo_copy(hsend, hrecv, k, counts[k], hs, hr).start)
    send_group(sbuf, rbuf, (0, 2), fs, fr)
    gather_some((6, 8))
    send_group(sbuf, rbuf, (6, 8), fs, fr)
    gather_some((1, 3))
    send_group(sbuf, rbuf, (1, 3), fs, fr)
    gather_some((5, 7))
    send_group(sbuf, rbuf, (5, 7), fs, fr)
    for load in loads[7:]:
        load.wait()
    row_id = lax.broadcasted_iota(jnp.int32, (16, 128), 0)
    lane_id = lax.broadcasted_iota(jnp.int32, (16, 128), 1)
    keep_i = jnp.where(neighbour(SIDES[0])[0], 1.0, 0.0)
    keep_j = jnp.where(neighbour(SIDES[2])[0], 1.0, 0.0)

    def plane(i, carry):
        own = [x_ref[f, i] for f in range(4)]
        a = cell_terms(*own[:3])
        last = i == 15
        after = jnp.minimum(i + 1, 15)
        total = list(carry)
        out_carry = None
        for n in range(3):
            t = t_ref[n, i]
            if n == 0:
                nxt = [jnp.where(last, hrecv[1, f], x_ref[f, after]) for f in range(4)]
                t = t * jnp.where(last, keep_i, 1.0)
            elif n == 1:
                nxt = [
                    jnp.where(row_id == 15, hrecv[3, f, pl.ds(i, 1), :], pltpu.roll(own[f], 15, 0))
                    for f in range(4)
                ]
                t = jnp.where(row_id == 15, t * keep_j, t)
            else:
                nxt = [pltpu.roll(own[f], 127, 1) for f in range(4)]
                t = jnp.where(lane_id == 127, 0.0, t)
            b = cell_terms(*nxt[:3])
            values, (ww, wo, wg) = face_terms(t, a, b, own[0], nxt[0], own[3], nxt[3])
            mw, mo, mgd = values[2:5]
            cond_ref[n, i] = mw + mo + mgd
            upper = block_rows(b, ww, wo, wg, -mw, -mo, -mgd)
            lower = block_rows(a, -ww, -wo, -wg, -mw, -mo, -mgd)
            for e in range(9):
                blocks[n, 0, e, i] = upper[e].astype(BF16)
                blocks[n, 1, e, i] = lower[e].astype(BF16)
            total = [x + y for x, y in zip(total, values)]
            below = lower_side(values)
            if n == 0:
                out_carry = below
            elif n == 1:
                for v in range(8):
                    shifted = jnp.where(row_id == 0, lowj[v, pl.ds(i, 1), :], pltpu.roll(below[v], 1, 0))
                    total[v] = total[v] + shifted
            else:
                total = [x + pltpu.roll(y, 1, 1) for x, y in zip(total, below)]
        for v in range(8):
            fa[v, i] = total[v]
        return out_carry

    def fault_terms(d):
        near = [sbuf[d, f] for f in range(4)]
        far = [rbuf[d, f] for f in range(4)]
        a, b = cell_terms(*near[:3]), cell_terms(*far[:3])
        values, (ww, wo, wg) = face_terms(ft_ref[d], a, b, near[0], far[0], near[3], far[3])
        mw, mo, mgd = values[2:5]
        fcond_ref[d] = mw + mo + mgd
        for v in range(8):
            chan[v, d] = values[v]
        for e, value in enumerate(block_rows(b, ww, wo, wg, -mw, -mo, -mgd)):
            fault_rows[e, pl.ds(pl.multiple_of(d * 8, 8), 8), :] = value

    def scatter(d, c, low, high):
        four = range(c, c + 4)
        put = lanes([hot_ones(hot(lane_ref[d, pl.ds(q, 1), :], 256)) for q in four])
        masks = [hot(row_ref[d, pl.ds(q, 1), :], 128) for q in four]
        his, los = [], []
        for v in range(low, high):
            both = [hot_low_values(m, chan[v, d, pl.ds(q, 1), :]) for m, q in zip(masks, four)]
            his.append(lanes([x[0] for x in both]))
            los.append(lanes([x[1] for x in both]))
        low_put = (put * jnp.asarray(LOW, BF16)).astype(F8)
        out = dot_slots(rows(his), put) + dot_slots(rows(los).astype(F8), low_put)
        acc[low * 128 : high * 128, :] += out

    def arrived(g, h):
        pair = [direction(g, h, u) for u in range(2)]
        wait_group(sbuf, rbuf, pair, fs, fr)
        for d in pair:
            fault_terms(d)

    def corner_half(h, carry):
        arrived(0, h)
        for u in range(2):
            for m in range(2):
                scatter(direction(0, h, u), 4 * m, 2, 8)
        return carry

    def side_half(h, carry):
        arrived(1, h)
        below = [carry_ref[v] for v in range(8)]
        for u in range(2):
            for m in range(2):
                scatter(direction(1, h, u), 4 * m, 2, 8)
                for n in range(2):
                    below = plane(h * 8 + u * 4 + m * 2 + n, below)
        for v in range(8):
            carry_ref[v] = below[v]
        return carry

    def scatter_drives(ds):
        for d in ds:
            for m in range(2):
                scatter(d, 4 * m, 0, 2)

    lax.fori_loop(0, 2, corner_half, 0)
    wait_halos(hsend, hrecv, counts, hs, hr)

    def low_face(k, fields):
        a = [hrecv[k, f] for f in range(4)]
        values, _ = face_terms(
            hrecv[k, 4], cell_terms(*a[:3]), cell_terms(*fields[:3]), a[0], fields[0], a[3], fields[3]
        )
        condlow_ref[k // 2] = values[2] + values[3] + values[4]
        return lower_side(values)

    for v, value in enumerate(low_face(2, [x_ref[f, :, 0, :] for f in range(4)])):
        lowj[v] = value
    for v, value in enumerate(low_face(0, [x_ref[f, 0] for f in range(4)])):
        carry_ref[v] = value
    lax.fori_loop(0, 2, side_half, 0)

    cell = pc_ref[...]
    row, lane = cell_rows(cell >> 7, cell & 127)
    mask = hot(row, 128)
    hi_w, lo_w = hot_values(mask, w_ref[0])
    hi_q, lo_q = hot_values(mask, w_ref[0] * w_ref[1])
    put = hot_ones(hot(lane, 256))
    wacc[...] = dot_slots(lanes([rows([hi_w, hi_q]), rows([lo_w, lo_q])]), lanes([put, put]))

    def sums(i, first, last):
        return [fa[v, i] + rows_of(acc, v * 128 + i * 8) for v in range(first, last)]

    def accumulation(i):
        p, sw, sg = x_ref[0, i], x_ref[1, i], x_ref[2, i]
        well = rows_of(wacc, i * 8)
        drive = rows_of(wacc, 128 + i * 8) - p * well
        oil = 1.0 - sw - sg
        pv = x_ref[4, i]
        rock = 2.0 * (pv * (1.0 + 0.02 * p))
        rock_p = 0.04 * pv
        bw, bo, bg, rs = 1.0 + 0.05 * p, 1.0 + 0.1 * p, 1.0 + 0.4 * p, 0.5 + 0.2 * p
        ob = oil * bo
        gas = sg * bg + rs * ob
        a0 = rock_p * sw * bw + rock * sw * 0.05
        a3 = rock_p * ob + rock * oil * 0.1
        a6 = rock_p * gas + rock * (0.4 * sg + 0.2 * ob + 0.1 * rs * oil)
        return cell_terms(p, sw, sg), well, drive, rock, (rock * sw * bw, rock * ob, rock * gas), (a0, a3, a6), (bw, bo, bg, rs)

    def residuals(i):
        mw, mo, mgd, rw, ro, rg = sums(i, 2, 8)
        c, well, drive, rock, held, slope, _ = accumulation(i)
        r0 = held[0] - 2.0 * om_ref[0, i] + rw - drive * c["mw"]
        r1 = held[1] - 2.0 * om_ref[1, i] + ro - drive * c["mo"]
        r2 = held[2] - 2.0 * om_ref[2, i] + rg - drive * (c["mg"] + c["md"])
        res_ref[0, i], res_ref[1, i], res_ref[2, i] = r0, r1, r2
        total = c["mw"] + c["mo"] + c["mg"] + c["md"]
        pd = slope[0] + slope[1] + slope[2] + mw + mo + mgd + well * total
        rhs = -(r0 + r1 + r2)
        rhs_ref[i] = rhs
        pd_ref[i] = pd
        first_ref[i] = rhs / pd

    def diagonals(i):
        hp, hz, mw, mo, mgd = sums(i, 0, 5)
        c, well, drive, rock, held, slope, (bw, bo, bg, rs) = accumulation(i)
        dw = hp - 0.1 * hz - drive
        do = hp - 0.08 * hz - drive
        dg = hp - 0.02 * hz - drive
        pair = -(rock * bo) - c["mo_o"] * do
        gas_water = -(rock * rs * bo) - c["md_o"] * do
        out = (
            slope[0] + c["mw_p"] * dw + mw + well * c["mw"],
            rock * bw + c["mw_s"] * dw,
            jnp.zeros_like(dw),
            slope[1] + c["mo_p"] * do + mo + well * c["mo"],
            pair,
            pair,
            slope[2] + c["mg_p"] * dg + c["md_p"] * do + mgd + well * (c["mg"] + c["md"]),
            gas_water,
            rock * bg + c["mg_s"] * dg + gas_water,
        )
        for e in range(9):
            diag_ref[e, i] = out[e].astype(BF16)

    plane_loop(residuals)
    hsend2[0, 0] = first_ref[15]
    hsend2[1, 0] = first_ref[0]
    hsend2[2, 0] = first_ref[:, 15, :]
    hsend2[3, 0] = first_ref[:, 0, :]
    for k in (2, 3, 0, 1):
        pl.when(neighbour(SIDES[k])[0])(halo_copy(hsend2, hrecv2, k, 1, hs2, hr2).start)
    hi, lo = split(as_rows(first_ref[...]))
    ghl[0:128, :] = hi
    ghl[128:256, :] = lo

    def gather_first(ds):
        for d in ds:

            def store(f, q, value):
                sbuf2[d, pl.ds(q, 1), :] = value

            gather([ghl[...]], 1, row_ref, lane_ref, d, store)
        send_group(sbuf2, rbuf2, ds, fs2, fr2)

    two_groups(gather_first)
    two_groups(scatter_drives)

    def fault_out(e, carry):
        for di in range(3):
            for q in range(8):
                line = fault_rows[e, pl.ds(di * 24 + q, 3, 8), :]
                fault_ref[e, 0, di, :, pl.ds(q * 128, 128)] = line.astype(BF16)
        return carry

    lax.fori_loop(0, 9, fault_out, 0)
    plane_loop(diagonals)
    acc2[...] = jnp.zeros_like(acc2)
    wait_group(sbuf2, rbuf2, group(0), fs2, fr2)
    scatter_first(group(0), row_ref, lane_ref, fcond_ref, rbuf2, acc2)
    wait_halos(hsend2, hrecv2, (1, 1, 1, 1), hs2, hr2)

    def faces(i):
        own = first_ref[i]
        before, after = jnp.maximum(i - 1, 0), jnp.minimum(i + 1, 15)
        up = jnp.where(i == 15, hrecv2[1, 0], first_ref[after])
        down = jnp.where(i == 0, hrecv2[0, 0], first_ref[before])
        total = cond_ref[0, i] * up
        total += jnp.where(i == 0, condlow_ref[0], cond_ref[0, before]) * down
        cj = cond_ref[1, i]
        up = jnp.where(row_id == 15, hrecv2[3, 0, pl.ds(i, 1), :], pltpu.roll(own, 15, 0))
        down = jnp.where(row_id == 0, hrecv2[2, 0, pl.ds(i, 1), :], pltpu.roll(own, 1, 0))
        cj_low = jnp.where(row_id == 0, condlow_ref[1, pl.ds(i, 1), :], pltpu.roll(cj, 1, 0))
        total += cj * up + cj_low * down
        ck = cond_ref[2, i]
        total += ck * pltpu.roll(own, 127, 1) + pltpu.roll(ck * own, 1, 1)
        at = pl.multiple_of(i * 8, 8)
        acc2[pl.ds(at, 8), 0:128] += total[0:8]
        acc2[pl.ds(at, 8), 128:256] += total[8:16]

    plane_loop(faces)
    wait_group(sbuf2, rbuf2, group(1), fs2, fr2)
    far2[...] = rbuf2[...]


def write_kernel(
    blocks, res_ref, diag_ref, fault_ref, rhs_ref, pd_ref, acc_in, far2, fcond_ref, row_ref, lane_ref,
    face_hbm, res_hbm, diag_hbm, fault_hbm, out_hbm,
    acc2, out_ref, sem,
):
    pairs = ((blocks, face_hbm), (diag_ref, diag_hbm), (res_ref, res_hbm), (fault_ref, fault_hbm), (out_ref, out_hbm))
    copies = [pltpu.make_async_copy(a, b, sem.at[n]) for n, (a, b) in enumerate(pairs)]
    for copy in copies[:4]:
        copy.start()
    acc2[...] = acc_in[...]
    scatter_first((1, 3, 5, 7), row_ref, lane_ref, fcond_ref, far2, acc2)

    def finish(i):
        at = pl.multiple_of(i * 8, 8)
        total = acc2[pl.ds(at, 8), :] + acc2[pl.ds(at + 128, 8), :]
        total = rows([total[:, 0:128], total[:, 128:256]])
        out_ref[i] = (rhs_ref[i] + total) / pd_ref[i]

    plane_loop(finish)
    copies[4].start()
    for copy in copies:
        copy.wait()


def in_vmem(count):
    return [pl.BlockSpec(memory_space=pltpu.VMEM)] * count


def in_hbm(count):
    return [pl.BlockSpec(memory_space=pltpu.HBM)] * count


def per_device(*args):
    p, fc = args[0], args[7]
    slots, cells = fc.shape[3], p.shape

    def placed(n, x):
        if n in (7, 8, 9):
            x = jnp.transpose(x, (1, 2, 0, 3)).reshape(9, 8, 128)
        return pltpu.with_memory_space_constraint(x, pltpu.HBM)

    def f32(*shape):
        return jax.ShapeDtypeStruct(shape, F32)

    def scratch(*shape, dtype=F32):
        return pltpu.VMEM(shape, dtype)

    dma = pltpu.SemaphoreType.DMA
    index = jax.ShapeDtypeStruct((9, 8, 128), jnp.int32)
    face = jax.ShapeDtypeStruct((3, 2, 9) + cells, BF16)
    diag = jax.ShapeDtypeStruct((9,) + cells, BF16)
    fault = jax.ShapeDtypeStruct((9, 1, 3, 3, slots), BF16)
    held = pl.pallas_call(
        system_kernel,
        out_shape=[
            face,
            f32(3, *cells),
            diag,
            fault,
            f32(*cells),
            f32(*cells),
            f32(256, 256),
            f32(9, 8, 128),
            f32(9, 8, 128),
            index,
            index,
        ],
        in_specs=in_hbm(13),
        out_specs=in_vmem(11),
        scratch_shapes=[
            scratch(5, *cells),
            scratch(3, *cells),
            scratch(3, *cells),
            scratch(9, 8, 128, dtype=jnp.int32),
            scratch(9, 8, 128, dtype=jnp.int32),
            scratch(9, 8, 128),
            scratch(1, 128, dtype=jnp.int32),
            scratch(2, 1, 128),
            scratch(9, 4, 8, 128),
            scratch(9, 4, 8, 128),
            scratch(4, 5, 16, 128),
            scratch(4, 5, 16, 128),
            scratch(512, 256, dtype=BF16),
            scratch(512, 256, dtype=BF16),
            scratch(8, 16, 128),
            scratch(8, 16, 128),
            scratch(1024, 256),
            scratch(8, *cells),
            scratch(256, 256),
            scratch(8, 9, 8, 128),
            scratch(9, 72, 128),
            scratch(3, *cells),
            scratch(2, 16, 128),
            scratch(*cells),
            scratch(9, 8, 128),
            scratch(9, 8, 128),
            scratch(4, 1, 16, 128),
            scratch(4, 1, 16, 128),
            scratch(256, 256, dtype=BF16),
            dma((13,)),
            dma((9,)),
            dma((9,)),
            dma((4,)),
            dma((4,)),
            dma((9,)),
            dma((9,)),
            dma((4,)),
            dma((4,)),
        ],
        compiler_params=pltpu.CompilerParams(
            collective_id=0, has_side_effects=True, vmem_limit_bytes=VMEM_BYTES
        ),
        name="system",
    )(*[placed(n, x) for n, x in enumerate(args)])
    face, res, diag, fault, update = pl.pallas_call(
        write_kernel,
        out_shape=[face, f32(3, *cells), diag, fault, f32(*cells)],
        in_specs=in_vmem(11),
        out_specs=in_hbm(5),
        scratch_shapes=[scratch(256, 256), scratch(*cells), dma((5,))],
        compiler_params=pltpu.CompilerParams(vmem_limit_bytes=VMEM_BYTES),
        name="write",
    )(*held)
    return res, diag, face, fault, update


def solution(mesh):
    cells = P("col", "row", None)
    stacked = P(None, "col", "row", None)
    owned = P(("col", "row"), None, None, None)
    wells = P(("col", "row"), None)
    return jax.shard_map(
        per_device,
        mesh=mesh,
        in_specs=(cells,) * 5 + (stacked,) * 2 + (owned,) * 3 + (wells,) * 3,
        out_specs=(
            stacked,
            stacked,
            P(None, None, None, "col", "row", None),
            P(None, ("col", "row"), None, None, None),
            cells,
        ),
        check_vma=False,
    )
```

```python
import jax
import jax.numpy as jnp
from jax import lax
from jax.experimental import pallas as pl
from jax.experimental.pallas import tpu as pltpu
from jax.sharding import PartitionSpec as P

F32 = jnp.float32
BF16 = jnp.bfloat16
F8 = jnp.float8_e4m3fn
LOW = 2.0**-6
MESH = pl.DeviceIdType.MESH
VMEM_BYTES = 40 * 1024 * 1024


def split(x):
    hi = x.astype(BF16)
    return hi, (x - hi.astype(F32)).astype(BF16)


def cell_terms(p, sw, sg):
    oil = 1.0 - sw - sg
    bw = 1.0 + 0.05 * p
    bo = 1.0 + 0.1 * p
    bg = 1.0 + 0.4 * p
    rs = 0.5 + 0.2 * p
    w2 = sw * (sw * (1.0 / 0.3))
    o2 = oil * (oil * (1.0 / 0.8))
    g2 = sg * (sg * (1.0 / 0.05))
    mo = bo * o2
    mo_p = 0.1 * o2
    mo_o = bo * (oil * (2.0 / 0.8))
    return dict(
        mw=bw * w2,
        mo=mo,
        mg=bg * g2,
        md=rs * mo,
        mw_p=0.05 * w2,
        mw_s=bw * (sw * (2.0 / 0.3)),
        mo_p=mo_p,
        mo_o=mo_o,
        mg_p=0.4 * g2,
        mg_s=bg * (sg * (2.0 / 0.05)),
        md_p=0.2 * mo + rs * mo_p,
        md_o=rs * mo_o,
    )


def face_terms(t, a, b, pa, pb, za, zb):
    half = 0.5 * t
    hp = half * (pa - pb)
    hz = half * (za - zb)
    ww = hp - 0.1 * hz
    wo = hp - 0.08 * hz
    wg = hp - 0.02 * hz
    sum_w = a["mw"] + b["mw"]
    sum_o = a["mo"] + b["mo"]
    sum_g = a["mg"] + b["mg"]
    sum_d = a["md"] + b["md"]
    mw = half * sum_w
    mo = half * sum_o
    mgd = half * (sum_g + sum_d)
    flux = (sum_w * ww, sum_o * wo, sum_g * wg + sum_d * wo)
    return (hp, hz, mw, mo, mgd) + flux, (ww, wo, wg)


def block_rows(c, ww, wo, wg, mw, mo, mgd):
    oil = c["mo_o"] * wo
    solved = c["md_o"] * wo
    zero = jnp.zeros_like(ww)
    return (
        c["mw_p"] * ww + mw,
        c["mw_s"] * ww,
        zero,
        c["mo_p"] * wo + mo,
        -oil,
        -oil,
        c["mg_p"] * wg + c["md_p"] * wo + mgd,
        -solved,
        c["mg_s"] * wg - solved,
    )


def neighbour(d):
    a, b = lax.axis_index("col"), lax.axis_index("row")
    ta, tb = a + d // 3 - 1, b + d % 3 - 1
    na, nb = lax.axis_size("col"), lax.axis_size("row")
    there = (ta >= 0) & (ta < na) & (tb >= 0) & (tb < nb)
    return there, (ta, tb)


def direction(g, h, u):
    return jnp.where(g == 0, 2 * u + 6 * h, 4 * h + 2 * u + 1)


def group(g):
    return [direction(g, h, u) for h in range(2) for u in range(2)]


def two_groups(body):
    def step(g, carry):
        body(group(g))
        return carry

    lax.fori_loop(0, 2, step, 0)


SIDES = (7, 1, 5, 3)


def greet():
    barrier = pltpu.get_barrier_semaphore()
    count = 0
    for d in (0, 1, 2, 3, 5, 6, 7, 8):
        there, target = neighbour(d)

        @pl.when(there)
        def _():
            pl.semaphore_signal(barrier, inc=1, device_id=target, device_id_type=MESH)

        count = count + there.astype(jnp.int32)
    return barrier, count


def halo_copy(src, dst, k, count, send_sem, recv_sem):
    return pltpu.make_async_remote_copy(
        src_ref=src.at[k, pl.ds(0, count)],
        dst_ref=dst.at[k, pl.ds(0, count)],
        send_sem=send_sem.at[k],
        recv_sem=recv_sem.at[k],
        device_id=neighbour(SIDES[k])[1],
        device_id_type=MESH,
    )


def fault_copy(src, dst, d, send_sem, recv_sem, back):
    return pltpu.make_async_remote_copy(
        src_ref=src.at[d],
        dst_ref=dst.at[back],
        send_sem=send_sem.at[d],
        recv_sem=recv_sem.at[back],
        device_id=neighbour(d)[1],
        device_id_type=MESH,
    )


def wait_halos(src, dst, counts, send_sem, recv_sem):
    for k in range(4):
        copy = halo_copy(src, dst, k, counts[k], send_sem, recv_sem)
        pl.when(neighbour(SIDES[k])[0])(copy.wait_send)
        pl.when(neighbour(8 - SIDES[k])[0])(copy.wait_recv)


def send_group(src, dst, ds, send_sem, recv_sem):
    for d in ds:
        pl.when(neighbour(d)[0])(fault_copy(src, dst, d, send_sem, recv_sem, 8 - d).start)


def wait_group(src, dst, ds, send_sem, recv_sem):
    for d in ds:
        copy = fault_copy(src, dst, d, send_sem, recv_sem, d)

        @pl.when(neighbour(d)[0])
        def _():
            copy.wait_send()
            copy.wait_recv()


def clear_missing(hrecv, rbuf):
    for k in range(4):

        @pl.when(jnp.logical_not(neighbour(8 - SIDES[k])[0]))
        def _():
            hrecv[k] = jnp.zeros_like(hrecv[k])

    def one(d, carry):
        @pl.when(jnp.logical_not(neighbour(d)[0]) | (d == 4))
        def _():
            rbuf[d] = jnp.zeros_like(rbuf[d])

        return carry

    lax.fori_loop(0, 9, one, 0)


def cell_rows(column, layer):
    return (column >> 4) * 8 + (column & 7), ((column >> 3) & 1) * 128 + layer


def hot(index, size):
    slots = index.shape[1]
    row = jnp.broadcast_to(index.astype(F32), (16, slots)).astype(BF16)
    iota = lax.broadcasted_iota(jnp.int32, (size, slots), 0).astype(F32).astype(BF16)
    return iota.reshape(size // 16, 16, slots) == row[None]


def hot_values(mask, value_row):
    slots = value_row.shape[1]
    hi, lo = split(jnp.broadcast_to(value_row, (16, slots)))
    zero = jnp.zeros((), BF16)
    return [jnp.where(mask, v[None], zero).reshape(128, slots) for v in (hi, lo)]


def hot_low_values(mask, value_row):
    slots = value_row.shape[1]
    value = jnp.broadcast_to(value_row, (16, slots))
    hi = value.astype(BF16)
    lo = ((value - hi.astype(F32)) * (1.0 / LOW)).astype(BF16)
    zero = jnp.zeros((), BF16)
    return [jnp.where(mask, v[None], zero).reshape(128, slots) for v in (hi, lo)]


def hot_ones(mask):
    size = mask.shape[0] * 16
    return jnp.where(mask, jnp.ones((), BF16), jnp.zeros((), BF16)).reshape(size, mask.shape[2])


def lanes(parts):
    return jnp.concatenate(parts, axis=1)


def rows(parts):
    return jnp.concatenate(parts, axis=0)


def as_rows(x):
    return lanes([x[:, 0:8, :].reshape(128, 128), x[:, 8:16, :].reshape(128, 128)])


def dot_slots(weighted, put):
    return lax.dot_general(weighted, put, (((1,), (1,)), ((), ())), preferred_element_type=F32)


def gather(pieces, count, row_ref, lane_ref, d, store):
    for c in range(0, 8, 2):
        pick = lanes([hot_ones(hot(lane_ref[d, pl.ds(q, 1), :], 256)) for q in (c, c + 1)])
        lines = None
        for piece in pieces:
            line = jnp.dot(piece, pick, preferred_element_type=F32)
            lines = line if lines is None else lines + line
        for s in range(2):
            mask = lax.broadcasted_iota(jnp.int32, (128, 128), 0) == row_ref[d, pl.ds(c + s, 1), :]
            for f in range(count):
                part = lines[f * 128 : (f + 1) * 128, s * 128 : (s + 1) * 128]
                if len(pieces) == 1:
                    at = (count + f) * 128
                    part = part + lines[at : at + 128, s * 128 : (s + 1) * 128]
                store(f, c + s, jnp.sum(jnp.where(mask, part, 0.0), axis=0, keepdims=True))


def lower_side(values):
    return (-values[0], -values[1], values[2], values[3], values[4]) + tuple(-v for v in values[5:])


def plane_loop(body):
    def step(i, carry):
        for n in range(4):
            body(4 * i + n)
        return carry

    lax.fori_loop(0, 4, step, 0)


def rows_of(ref, start):
    at = pl.multiple_of(start, 8)
    return rows([ref[pl.ds(at, 8), 0:128], ref[pl.ds(at, 8), 128:256]])


def scatter_first(ds, row_ref, lane_ref, fcond_ref, far_ref, acc2):
    for d in ds:
        values = fcond_ref[d] * far_ref[d]
        for c in range(0, 8, 2):
            pair = (c, c + 1)
            put = lanes([hot_ones(hot(lane_ref[d, pl.ds(q, 1), :], 256)) for q in pair])
            both = [hot_values(hot(row_ref[d, pl.ds(q, 1), :], 128), values[q : q + 1]) for q in pair]
            weighted = rows([lanes([x[0] for x in both]), lanes([x[1] for x in both])])
            acc2[...] += dot_slots(weighted, put)


def system_kernel(
    p_hbm, sw_hbm, sg_hbm, z_hbm, pv_hbm, om_hbm, t_hbm, fc_hbm, fl_hbm, ft_hbm, pc_hbm, wi_hbm, wp_hbm,
    blocks, res_ref, diag_ref, fault_ref, rhs_ref, pd_ref, acc2, far2, fcond_ref, row_ref, lane_ref,
    x_ref, t_ref, om_ref, fc_ref, fl_ref, ft_ref, pc_ref, w_ref, sbuf, rbuf, hsend, hrecv, ghi, glo, lowj,
    carry_ref, acc, fa, wacc, chan, fault_rows, cond_ref, condlow_ref, first_ref, sbuf2, rbuf2, hsend2, hrecv2, ghl,
    in_sem, fs, fr, hs, hr, fs2, fr2, hs2, hr2,
):
    barrier, count = greet()
    pairs = [(fc_hbm, fc_ref), (fl_hbm, fl_ref)]
    pairs += [(ref, x_ref.at[f]) for f, ref in enumerate((p_hbm, sw_hbm, sg_hbm, z_hbm))]
    pairs += [(t_hbm, t_ref), (ft_hbm, ft_ref), (pc_hbm, pc_ref), (wi_hbm, w_ref.at[0]), (wp_hbm, w_ref.at[1])]
    pairs += [(pv_hbm, x_ref.at[4]), (om_hbm, om_ref)]
    loads = [pltpu.make_async_copy(a, b, in_sem.at[n]) for n, (a, b) in enumerate(pairs)]
    for load in loads:
        load.start()
    clear_missing(hrecv, rbuf)
    clear_missing(hrecv2, rbuf2)
    fault_rows[:, 32:40, :] = jnp.zeros((9, 8, 128), F32)
    fcond_ref[4] = jnp.zeros((8, 128), F32)
    acc[...] = jnp.zeros_like(acc)
    for load in loads[:2]:
        load.wait()
    row, lane = cell_rows(fc_ref[...], fl_ref[...])
    row_ref[...] = row
    lane_ref[...] = lane
    for load in loads[2:6]:
        load.wait()
    for f in range(4):
        hi, lo = split(as_rows(x_ref[f]))
        ghi[pl.ds(f * 128, 128), :] = hi
        glo[pl.ds(f * 128, 128), :] = lo
    counts = (5, 4, 5, 4)

    def gather_some(ds):
        for d in ds:

            def store(f, q, value):
                sbuf[d, f, pl.ds(q, 1), :] = value

            gather([ghi[...], glo[...]], 4, row_ref, lane_ref, d, store)

    gather_some((0, 2))
    for f in range(4):
        hsend[0, f] = x_ref[f, 15]
        hsend[1, f] = x_ref[f, 0]
        hsend[2, f] = x_ref[f, :, 15, :]
        hsend[3, f] = x_ref[f, :, 0, :]
    loads[6].wait()
    hsend[0, 4] = t_ref[0, 15]
    hsend[2, 4] = t_ref[1, :, 15, :]
    pl.semaphore_wait(barrier, count)
    for k in (2, 3, 0, 1):
        pl.when(neighbour(SIDES[k])[0])(halo_copy(hsend, hrecv, k, counts[k], hs, hr).start)
    send_group(sbuf, rbuf, (0, 2), fs, fr)
    gather_some((6, 8))
    send_group(sbuf, rbuf, (6, 8), fs, fr)
    gather_some((1, 3))
    send_group(sbuf, rbuf, (1, 3), fs, fr)
    gather_some((5, 7))
    send_group(sbuf, rbuf, (5, 7), fs, fr)
    for load in loads[7:]:
        load.wait()
    row_id = lax.broadcasted_iota(jnp.int32, (16, 128), 0)
    lane_id = lax.broadcasted_iota(jnp.int32, (16, 128), 1)
    keep_i = jnp.where(neighbour(SIDES[0])[0], 1.0, 0.0)
    keep_j = jnp.where(neighbour(SIDES[2])[0], 1.0, 0.0)

    def plane(i, carry):
        own = [x_ref[f, i] for f in range(4)]
        a = cell_terms(*own[:3])
        last = i == 15
        after = jnp.minimum(i + 1, 15)
        total = list(carry)
        out_carry = None
        for n in range(3):
            t = t_ref[n, i]
            if n == 0:
                nxt = [jnp.where(last, hrecv[1, f], x_ref[f, after]) for f in range(4)]
                t = t * jnp.where(last, keep_i, 1.0)
            elif n == 1:
                nxt = [
                    jnp.where(row_id == 15, hrecv[3, f, pl.ds(i, 1), :], pltpu.roll(own[f], 15, 0))
                    for f in range(4)
                ]
                t = jnp.where(row_id == 15, t * keep_j, t)
            else:
                nxt = [pltpu.roll(own[f], 127, 1) for f in range(4)]
                t = jnp.where(lane_id == 127, 0.0, t)
            b = cell_terms(*nxt[:3])
            values, (ww, wo, wg) = face_terms(t, a, b, own[0], nxt[0], own[3], nxt[3])
            mw, mo, mgd = values[2:5]
            cond_ref[n, i] = mw + mo + mgd
            upper = block_rows(b, ww, wo, wg, -mw, -mo, -mgd)
            lower = block_rows(a, -ww, -wo, -wg, -mw, -mo, -mgd)
            for e in range(9):
                blocks[n, 0, e, i] = upper[e].astype(BF16)
                blocks[n, 1, e, i] = lower[e].astype(BF16)
            total = [x + y for x, y in zip(total, values)]
            below = lower_side(values)
            if n == 0:
                out_carry = below
            elif n == 1:
                for v in range(8):
                    shifted = jnp.where(row_id == 0, lowj[v, pl.ds(i, 1), :], pltpu.roll(below[v], 1, 0))
                    total[v] = total[v] + shifted
            else:
                total = [x + pltpu.roll(y, 1, 1) for x, y in zip(total, below)]
        for v in range(8):
            fa[v, i] = total[v]
        return out_carry

    def fault_terms(d):
        near = [sbuf[d, f] for f in range(4)]
        far = [rbuf[d, f] for f in range(4)]
        a, b = cell_terms(*near[:3]), cell_terms(*far[:3])
        values, (ww, wo, wg) = face_terms(ft_ref[d], a, b, near[0], far[0], near[3], far[3])
        mw, mo, mgd = values[2:5]
        fcond_ref[d] = mw + mo + mgd
        for v in range(8):
            chan[v, d] = values[v]
        for e, value in enumerate(block_rows(b, ww, wo, wg, -mw, -mo, -mgd)):
            fault_rows[e, pl.ds(pl.multiple_of(d * 8, 8), 8), :] = value

    def scatter(d, c, low, high):
        four = range(c, c + 4)
        put = lanes([hot_ones(hot(lane_ref[d, pl.ds(q, 1), :], 256)) for q in four])
        masks = [hot(row_ref[d, pl.ds(q, 1), :], 128) for q in four]
        his, los = [], []
        for v in range(low, high):
            both = [hot_low_values(m, chan[v, d, pl.ds(q, 1), :]) for m, q in zip(masks, four)]
            his.append(lanes([x[0] for x in both]))
            los.append(lanes([x[1] for x in both]))
        low_put = (put * jnp.asarray(LOW, BF16)).astype(F8)
        out = dot_slots(rows(his), put) + dot_slots(rows(los).astype(F8), low_put)
        acc[low * 128 : high * 128, :] += out

    def arrived(g, h):
        pair = [direction(g, h, u) for u in range(2)]
        wait_group(sbuf, rbuf, pair, fs, fr)
        for d in pair:
            fault_terms(d)

    def corner_half(h, carry):
        arrived(0, h)
        for u in range(2):
            for m in range(2):
                scatter(direction(0, h, u), 4 * m, 2, 8)
        return carry

    def side_half(h, carry):
        arrived(1, h)
        below = [carry_ref[v] for v in range(8)]
        for u in range(2):
            for m in range(2):
                scatter(direction(1, h, u), 4 * m, 2, 8)
                for n in range(2):
                    below = plane(h * 8 + u * 4 + m * 2 + n, below)
        for v in range(8):
            carry_ref[v] = below[v]
        return carry

    def scatter_drives(ds):
        for d in ds:
            for m in range(2):
                scatter(d, 4 * m, 0, 2)

    lax.fori_loop(0, 2, corner_half, 0)
    wait_halos(hsend, hrecv, counts, hs, hr)

    def low_face(k, fields):
        a = [hrecv[k, f] for f in range(4)]
        values, _ = face_terms(
            hrecv[k, 4], cell_terms(*a[:3]), cell_terms(*fields[:3]), a[0], fields[0], a[3], fields[3]
        )
        condlow_ref[k // 2] = values[2] + values[3] + values[4]
        return lower_side(values)

    for v, value in enumerate(low_face(2, [x_ref[f, :, 0, :] for f in range(4)])):
        lowj[v] = value
    for v, value in enumerate(low_face(0, [x_ref[f, 0] for f in range(4)])):
        carry_ref[v] = value
    lax.fori_loop(0, 2, side_half, 0)

    cell = pc_ref[...]
    row, lane = cell_rows(cell >> 7, cell & 127)
    mask = hot(row, 128)
    hi_w, lo_w = hot_values(mask, w_ref[0])
    hi_q, lo_q = hot_values(mask, w_ref[0] * w_ref[1])
    put = hot_ones(hot(lane, 256))
    wacc[...] = dot_slots(lanes([rows([hi_w, hi_q]), rows([lo_w, lo_q])]), lanes([put, put]))

    def sums(i, first, last):
        return [fa[v, i] + rows_of(acc, v * 128 + i * 8) for v in range(first, last)]

    def accumulation(i):
        p, sw, sg = x_ref[0, i], x_ref[1, i], x_ref[2, i]
        well = rows_of(wacc, i * 8)
        drive = rows_of(wacc, 128 + i * 8) - p * well
        oil = 1.0 - sw - sg
        pv = x_ref[4, i]
        rock = 2.0 * (pv * (1.0 + 0.02 * p))
        rock_p = 0.04 * pv
        bw, bo, bg, rs = 1.0 + 0.05 * p, 1.0 + 0.1 * p, 1.0 + 0.4 * p, 0.5 + 0.2 * p
        ob = oil * bo
        gas = sg * bg + rs * ob
        a0 = rock_p * sw * bw + rock * sw * 0.05
        a3 = rock_p * ob + rock * oil * 0.1
        a6 = rock_p * gas + rock * (0.4 * sg + 0.2 * ob + 0.1 * rs * oil)
        return cell_terms(p, sw, sg), well, drive, rock, (rock * sw * bw, rock * ob, rock * gas), (a0, a3, a6), (bw, bo, bg, rs)

    def residuals(i):
        mw, mo, mgd, rw, ro, rg = sums(i, 2, 8)
        c, well, drive, rock, held, slope, _ = accumulation(i)
        r0 = held[0] - 2.0 * om_ref[0, i] + rw - drive * c["mw"]
        r1 = held[1] - 2.0 * om_ref[1, i] + ro - drive * c["mo"]
        r2 = held[2] - 2.0 * om_ref[2, i] + rg - drive * (c["mg"] + c["md"])
        res_ref[0, i], res_ref[1, i], res_ref[2, i] = r0, r1, r2
        total = c["mw"] + c["mo"] + c["mg"] + c["md"]
        pd = slope[0] + slope[1] + slope[2] + mw + mo + mgd + well * total
        rhs = -(r0 + r1 + r2)
        rhs_ref[i] = rhs
        pd_ref[i] = pd
        first_ref[i] = rhs / pd

    def diagonals(i):
        hp, hz, mw, mo, mgd = sums(i, 0, 5)
        c, well, drive, rock, held, slope, (bw, bo, bg, rs) = accumulation(i)
        dw = hp - 0.1 * hz - drive
        do = hp - 0.08 * hz - drive
        dg = hp - 0.02 * hz - drive
        pair = -(rock * bo) - c["mo_o"] * do
        gas_water = -(rock * rs * bo) - c["md_o"] * do
        out = (
            slope[0] + c["mw_p"] * dw + mw + well * c["mw"],
            rock * bw + c["mw_s"] * dw,
            jnp.zeros_like(dw),
            slope[1] + c["mo_p"] * do + mo + well * c["mo"],
            pair,
            pair,
            slope[2] + c["mg_p"] * dg + c["md_p"] * do + mgd + well * (c["mg"] + c["md"]),
            gas_water,
            rock * bg + c["mg_s"] * dg + gas_water,
        )
        for e in range(9):
            diag_ref[e, i] = out[e].astype(BF16)

    plane_loop(residuals)
    hsend2[0, 0] = first_ref[15]
    hsend2[1, 0] = first_ref[0]
    hsend2[2, 0] = first_ref[:, 15, :]
    hsend2[3, 0] = first_ref[:, 0, :]
    for k in (2, 3, 0, 1):
        pl.when(neighbour(SIDES[k])[0])(halo_copy(hsend2, hrecv2, k, 1, hs2, hr2).start)
    hi, lo = split(as_rows(first_ref[...]))
    ghl[0:128, :] = hi
    ghl[128:256, :] = lo

    def gather_first(ds):
        for d in ds:

            def store(f, q, value):
                sbuf2[d, pl.ds(q, 1), :] = value

            gather([ghl[...]], 1, row_ref, lane_ref, d, store)
        send_group(sbuf2, rbuf2, ds, fs2, fr2)

    two_groups(gather_first)
    two_groups(scatter_drives)

    def fault_out(e, carry):
        for di in range(3):
            for q in range(8):
                line = fault_rows[e, pl.ds(di * 24 + q, 3, 8), :]
                fault_ref[e, 0, di, :, pl.ds(q * 128, 128)] = line.astype(BF16)
        return carry

    lax.fori_loop(0, 9, fault_out, 0)
    plane_loop(diagonals)
    acc2[...] = jnp.zeros_like(acc2)
    wait_group(sbuf2, rbuf2, group(0), fs2, fr2)
    scatter_first(group(0), row_ref, lane_ref, fcond_ref, rbuf2, acc2)
    wait_halos(hsend2, hrecv2, (1, 1, 1, 1), hs2, hr2)

    def faces(i):
        own = first_ref[i]
        before, after = jnp.maximum(i - 1, 0), jnp.minimum(i + 1, 15)
        up = jnp.where(i == 15, hrecv2[1, 0], first_ref[after])
        down = jnp.where(i == 0, hrecv2[0, 0], first_ref[before])
        total = cond_ref[0, i] * up
        total += jnp.where(i == 0, condlow_ref[0], cond_ref[0, before]) * down
        cj = cond_ref[1, i]
        up = jnp.where(row_id == 15, hrecv2[3, 0, pl.ds(i, 1), :], pltpu.roll(own, 15, 0))
        down = jnp.where(row_id == 0, hrecv2[2, 0, pl.ds(i, 1), :], pltpu.roll(own, 1, 0))
        cj_low = jnp.where(row_id == 0, condlow_ref[1, pl.ds(i, 1), :], pltpu.roll(cj, 1, 0))
        total += cj * up + cj_low * down
        ck = cond_ref[2, i]
        total += ck * pltpu.roll(own, 127, 1) + pltpu.roll(ck * own, 1, 1)
        at = pl.multiple_of(i * 8, 8)
        acc2[pl.ds(at, 8), 0:128] += total[0:8]
        acc2[pl.ds(at, 8), 128:256] += total[8:16]

    plane_loop(faces)
    wait_group(sbuf2, rbuf2, group(1), fs2, fr2)
    far2[...] = rbuf2[...]


def write_kernel(
    blocks, res_ref, diag_ref, fault_ref, rhs_ref, pd_ref, acc_in, far2, fcond_ref, row_ref, lane_ref,
    face_hbm, res_hbm, diag_hbm, fault_hbm, out_hbm,
    acc2, out_ref, sem,
):
    pairs = ((blocks, face_hbm), (diag_ref, diag_hbm), (res_ref, res_hbm), (fault_ref, fault_hbm), (out_ref, out_hbm))
    copies = [pltpu.make_async_copy(a, b, sem.at[n]) for n, (a, b) in enumerate(pairs)]
    for copy in copies[:4]:
        copy.start()
    acc2[...] = acc_in[...]
    scatter_first((1, 3, 5, 7), row_ref, lane_ref, fcond_ref, far2, acc2)

    def finish(i):
        at = pl.multiple_of(i * 8, 8)
        total = acc2[pl.ds(at, 8), :] + acc2[pl.ds(at + 128, 8), :]
        total = rows([total[:, 0:128], total[:, 128:256]])
        out_ref[i] = (rhs_ref[i] + total) / pd_ref[i]

    plane_loop(finish)
    copies[4].start()
    for copy in copies:
        copy.wait()


def in_vmem(count):
    return [pl.BlockSpec(memory_space=pltpu.VMEM)] * count


def in_hbm(count):
    return [pl.BlockSpec(memory_space=pltpu.HBM)] * count


def per_device(*args):
    p, fc = args[0], args[7]
    slots, cells = fc.shape[3], p.shape

    def placed(n, x):
        if n in (7, 8, 9):
            x = jnp.transpose(x, (1, 2, 0, 3)).reshape(9, 8, 128)
        return pltpu.with_memory_space_constraint(x, pltpu.HBM)

    def f32(*shape):
        return jax.ShapeDtypeStruct(shape, F32)

    def scratch(*shape, dtype=F32):
        return pltpu.VMEM(shape, dtype)

    dma = pltpu.SemaphoreType.DMA
    index = jax.ShapeDtypeStruct((9, 8, 128), jnp.int32)
    face = jax.ShapeDtypeStruct((3, 2, 9) + cells, BF16)
    diag = jax.ShapeDtypeStruct((9,) + cells, BF16)
    fault = jax.ShapeDtypeStruct((9, 1, 3, 3, slots), BF16)
    held = pl.pallas_call(
        system_kernel,
        out_shape=[
            face,
            f32(3, *cells),
            diag,
            fault,
            f32(*cells),
            f32(*cells),
            f32(256, 256),
            f32(9, 8, 128),
            f32(9, 8, 128),
            index,
            index,
        ],
        in_specs=in_hbm(13),
        out_specs=in_vmem(11),
        scratch_shapes=[
            scratch(5, *cells),
            scratch(3, *cells),
            scratch(3, *cells),
            scratch(9, 8, 128, dtype=jnp.int32),
            scratch(9, 8, 128, dtype=jnp.int32),
            scratch(9, 8, 128),
            scratch(1, 128, dtype=jnp.int32),
            scratch(2, 1, 128),
            scratch(9, 4, 8, 128),
            scratch(9, 4, 8, 128),
            scratch(4, 5, 16, 128),
            scratch(4, 5, 16, 128),
            scratch(512, 256, dtype=BF16),
            scratch(512, 256, dtype=BF16),
            scratch(8, 16, 128),
            scratch(8, 16, 128),
            scratch(1024, 256),
            scratch(8, *cells),
            scratch(256, 256),
            scratch(8, 9, 8, 128),
            scratch(9, 72, 128),
            scratch(3, *cells),
            scratch(2, 16, 128),
            scratch(*cells),
            scratch(9, 8, 128),
            scratch(9, 8, 128),
            scratch(4, 1, 16, 128),
            scratch(4, 1, 16, 128),
            scratch(256, 256, dtype=BF16),
            dma((13,)),
            dma((9,)),
            dma((9,)),
            dma((4,)),
            dma((4,)),
            dma((9,)),
            dma((9,)),
            dma((4,)),
            dma((4,)),
        ],
        compiler_params=pltpu.CompilerParams(
            collective_id=0, has_side_effects=True, vmem_limit_bytes=VMEM_BYTES
        ),
        name="system",
    )(*[placed(n, x) for n, x in enumerate(args)])
    face, res, diag, fault, update = pl.pallas_call(
        write_kernel,
        out_shape=[face, f32(3, *cells), diag, fault, f32(*cells)],
        in_specs=in_vmem(11),
        out_specs=in_hbm(5),
        scratch_shapes=[scratch(256, 256), scratch(*cells), dma((5,))],
        compiler_params=pltpu.CompilerParams(vmem_limit_bytes=VMEM_BYTES),
        name="write",
    )(*held)
    return res, diag, face, fault, update


def solution(mesh):
    cells = P("col", "row", None)
    stacked = P(None, "col", "row", None)
    owned = P(("col", "row"), None, None, None)
    wells = P(("col", "row"), None)
    return jax.shard_map(
        per_device,
        mesh=mesh,
        in_specs=(cells,) * 5 + (stacked,) * 2 + (owned,) * 3 + (wells,) * 3,
        out_specs=(
            stacked,
            stacked,
            P(None, None, None, "col", "row", None),
            P(None, ("col", "row"), None, None, None),
            cells,
        ),
        check_vma=False,
    )
```
